512 devices in a mesh: dp: 32 (over z_lo, x, core), tensor: 16 (over y, z_hi).
Axes of the slice: x: 4, y: 8, z: 8 (z_hi: 2, z_lo: 4; z = z_hi * 4 + z_lo), core: 2. Of those that a mesh axis runs over, the one named last changes fastest.
Arguments:
- x_input: bfloat16 [8192, 4096], P('dp', 'tensor'), may hold values from -6 to 6
- z_input: bfloat16 [8192, 4096], P('dp', 'tensor'), may hold values from -8 to 8
- dt_raw: float32 [64, 8192], P('tensor', 'dp'), may hold values from -5 to 5
- b_rows: bfloat16 [8192, 128], P(('dp', 'tensor')), may hold values from -2 to 2
- c_rows: bfloat16 [8192, 128], P(('dp', 'tensor')), may hold values from -2 to 2
- a_log: float32 [64], P('tensor'), may hold values from -4 to 1
- skip_gain: float32 [64], P('tensor'), may hold values from 0.5 to 2
- dt_bias: float32 [64], P('tensor'), may hold values from -3 to 0
- norm_gain: float32 [4096], P('tensor'), may hold values from 0.5 to 1.5
- w_out: bfloat16 [4096, 2048], P('tensor'), may hold values from -0.09375 to 0.09375
- grad_rows: bfloat16 [8192, 2048], P(('dp', 'tensor')), may hold values from -6 to 6
- doc_ids: int32 [8192], P('dp'), may hold values from 0 to 255, never falling along the last dimension, each value on 1 to 64 neighbouring positions
Outputs:
- grad_x: bfloat16 [8192, 4096], P('dp', 'tensor')
- grad_z: bfloat16 [8192, 4096], P('dp', 'tensor')
- grad_dt: float32 [64, 8192], P('tensor', 'dp')
- grad_b: float32 [8192, 128], P(('dp', 'tensor'))
- grad_c: float32 [8192, 128], P(('dp', 'tensor'))
- grad_w_out: bfloat16 [4096, 2048], P('tensor')
- grad_norm: float32 [4096], P('tensor')
- grad_a_log: float32 [64], P('tensor')
- grad_skip: float32 [64], P('tensor')
- grad_dt_bias: float32 [64], P('tensor')
The draws below stay inside these ranges and needn't reach their ends.
Inputs may be any that keep to these rules, and one draw needn't show every extreme that they name: `doc_ids`: ids never fall along the tokens; a document has at most 64 tokens.
All inputs are finite; a program needn't handle non-finite values.
Results may differ from the reference program's by a relative error of at most 0.025.
Values may be sent and summed in bfloat16 or wider, within the bound.
A program may use at most 64 MiB of HBM per device.

```python
import math
import jax
import jax.numpy as jnp
import numpy as np
from jax import lax

D = 2048
N = 128
SPAN = 128
DOCS = 8
SEQ = 256
HEADS = 64
INNER = 4096
TOKENS = 8192
N_DP = 32


def block_levels(rng, extent, pieces, low, largest):
    def one(dim, blocks):
        heights = jax.random.uniform(jax.random.fold_in(jax.random.fold_in(rng, 6), dim), (blocks,), jnp.float32, low / len(pieces), largest / len(pieces))
        return jnp.repeat(jnp.exp(heights), extent[dim] // blocks).reshape((-1,) + (1,) * (len(extent) - dim - 1))

    level = one(*pieces[0])
    for cut in pieces[1:]:
        level = level * one(*cut)
    return level


def profile(amount, total, limit, lean):
    portions = [(1 << 20) // math.isqrt(rank ** lean) + 1 for rank in range(2, amount + 1)]
    spare, given = total - limit - (amount - 1), [1] * (amount - 1)
    while spare > 0:
        free = [i for i in range(amount - 1) if given[i] < limit]
        whole, remaining = sum([portions[i] for i in free]), spare
        for i in free:
            extra = min(limit - given[i], max(1, remaining * portions[i] // whole), spare)
            given[i] = given[i] + extra
            spare = spare - extra
    return np.array([limit] + given)


def ragged(rng, number_of, total, reach, skew):
    if number_of == 2:
        one = jax.random.randint(rng, (), max(1, total - reach), min(reach, total - 1) + 1)
        return jnp.stack([one, total - one])
    sizes = jnp.asarray(profile(number_of, total, reach, skew), jnp.int32)
    couples = (number_of - 1) // 2
    donor, receiver = sizes[1:1 + 2 * couples:2], sizes[2:2 + 2 * couples:2]
    margin = jnp.minimum(donor - 1, reach - receiver)
    passed = jax.random.randint(jax.random.fold_in(rng, 1), (couples,), 0, 1 << 20) % (margin + 1)
    sizes = sizes.at[1:1 + 2 * couples:2].set(donor - passed).at[2:2 + 2 * couples:2].set(receiver + passed)
    return sizes[jax.random.permutation(jax.random.fold_in(rng, 2), number_of)]


def normal_values(own_key, shape, scale, most, split=(), held_as=jnp.bfloat16):
    level = block_levels(own_key, shape, split, -0.22, 0.18) if split else 1.0
    values = jax.random.normal(own_key, shape, jnp.float32) * scale * level
    return jnp.minimum(jnp.maximum(values, -most), most).astype(held_as)


def setup_inputs(seed: int = 0) -> dict:
    keys = jax.random.split(jax.random.key(seed), 13)
    x_input = normal_values(keys[0], (TOKENS, INNER), 1.0, 6.0, ((0, 32), (1, 16)))
    z_input = normal_values(keys[1], (TOKENS, INNER), 1.5, 8.0, ((0, 32), (1, 16)))
    dt_raw = normal_values(keys[2], (HEADS, TOKENS), 1.0, 5.0, ((0, 16), (1, 32)), jnp.float32)
    b_rows = normal_values(keys[3], (TOKENS, N), 0.3, 2.0, ((0, 512),))
    c_rows = normal_values(keys[4], (TOKENS, N), 0.3, 2.0, ((0, 512),))
    a_log = jnp.clip(-4.0 + 5.0 * jax.random.uniform(keys[5], (HEADS,), jnp.float32) ** block_levels(keys[5], (HEADS,), ((0, 16),), -0.2, 0.2), -4.0, 1.0)
    skip_gain = jnp.clip(0.5 + 1.5 * jax.random.uniform(keys[6], (HEADS,), jnp.float32) ** block_levels(keys[6], (HEADS,), ((0, 16),), -0.2, 0.2), 0.5, 2.0)
    dt_bias = jnp.clip(-3.0 + 3.0 * jax.random.uniform(keys[7], (HEADS,), jnp.float32) ** block_levels(keys[7], (HEADS,), ((0, 16),), -0.2, 0.2), -3.0, 0.0)
    norm_gain = jnp.clip(1.0 + 0.1 * jax.random.normal(keys[8], (INNER,), jnp.float32), 0.5, 1.5)
    w_out = normal_values(keys[9], (INNER, D), INNER ** -0.5, 0.09375, ((0, 16),))
    grad_rows = normal_values(keys[10], (TOKENS, D), 1.0, 6.0, ((0, 512),))
    doc_ids = jnp.searchsorted(jnp.cumsum(ragged(keys[11], DOCS * N_DP, TOKENS, SEQ // 4, 1)), jnp.arange(TOKENS), side="right").astype(jnp.int32)
    return dict(x_input=x_input, z_input=z_input, dt_raw=dt_raw, b_rows=b_rows, c_rows=c_rows, a_log=a_log, skip_gain=skip_gain, dt_bias=dt_bias, norm_gain=norm_gain, w_out=w_out, grad_rows=grad_rows, doc_ids=doc_ids)


epsilon = 1e-05
exact = lax.Precision.HIGHEST

def ssd_gate(x_all, z_all, dt_raw, b_all, c_all, a_log, skip_gain, dt_bias, doc_ids, span):
    seqlen = x_all.shape[0]
    nheads = dt_raw.shape[0]
    head_size = x_all.shape[1] // nheads
    blocks = seqlen // span
    low = jnp.bfloat16
    wide = jnp.float32
    step_size = jax.nn.softplus(dt_raw + dt_bias[:, None])
    log_decay = -jnp.exp(a_log)[:, None] * step_size
    cum_decay = jnp.cumsum(log_decay.reshape(nheads, blocks, span), axis=2)
    seg_blocks = doc_ids.reshape(blocks, span).astype(jnp.int32)
    prev_seg = jnp.concatenate([jnp.full((1,), -1, jnp.int32), seg_blocks[:-1, -1].astype(jnp.int32)])
    causal = jnp.arange(span)[:, None] >= jnp.arange(span)[None, :]
    same_doc = (causal[None] & (seg_blocks[:, :, None] == seg_blocks[:, None, :])).astype(jnp.float32)
    log_gap = cum_decay[:, :, :, None] - cum_decay[:, :, None, :]
    decay_in = jnp.exp(jnp.minimum(log_gap, 0.0)) * same_doc[None]
    step_blocks = step_size.reshape(nheads, blocks, span)
    x_heads = x_all.reshape(blocks, span, nheads, head_size)
    x_low = x_heads.astype(low)
    b_low = b_all.reshape(blocks, span, -1).astype(low)
    c_low = c_all.reshape(blocks, span, -1).astype(low)
    scores = jnp.einsum('cin,cjn->cij', c_low, b_low, preferred_element_type=wide, precision=exact)
    mixing = decay_in * scores[None] * step_blocks[:, :, None, :]
    y_intra = jnp.einsum('hcij,cjhp->cihp', mixing.astype(low), x_low, preferred_element_type=wide, precision=exact)
    end_mask = (seg_blocks[:, -1:] == seg_blocks).astype(jnp.float32)
    to_end = jnp.exp(cum_decay[:, :, -1:] - cum_decay) * end_mask[None] * step_blocks
    weighted = x_heads * to_end.transpose(1, 2, 0)[:, :, :, None]
    states = jnp.einsum('cjhp,cjn->chpn', weighted.astype(low), b_low, preferred_element_type=wide, precision=exact)
    carry_mask = (seg_blocks[:, -1] == prev_seg).astype(jnp.float32)
    carry_decay = jnp.exp(cum_decay[:, :, -1]) * carry_mask[None]

    def advance(state, inputs):
        block_state, block_decay = inputs
        return (block_decay[:, None, None] * state + block_state, state)
    _, entering = lax.scan(advance, jnp.zeros(states.shape[1:], jnp.float32), (states, carry_decay.T))
    start_mask = (seg_blocks == prev_seg[:, None]).astype(jnp.float32)
    from_start = jnp.exp(cum_decay) * start_mask[None]
    y_inter = jnp.einsum('cin,chpn->cihp', c_low, entering.astype(low), preferred_element_type=wide, precision=exact) * from_start.transpose(1, 2, 0)[:, :, :, None]
    outputs = y_intra + y_inter + skip_gain[None, None, :, None] * x_heads
    gate_in = z_all.reshape(blocks, span, nheads, head_size)
    gated = outputs * jax.nn.silu(gate_in)
    return gated.reshape(seqlen, nheads * head_size)

def group_grads(x_input, z_input, dt_raw, b_rows, c_rows, a_log, skip_gain, dt_bias, norm_gain, w_out, grad_rows, doc_ids):

    def core(x_all, z_all, dt_all, b_all, c_all, a_all, skip_all, bias_all):
        return ssd_gate(x_all, z_all, dt_all, b_all, c_all, a_all, skip_all, bias_all, doc_ids, SPAN)
    gated, pull = jax.vjp(core, x_input.astype(jnp.float32), z_input.astype(jnp.float32), dt_raw, b_rows.astype(jnp.float32), c_rows.astype(jnp.float32), a_log, skip_gain, dt_bias)
    channels = gated.shape[1]
    inv_rms = lax.rsqrt(lax.optimization_barrier(jnp.sum(gated * gated, axis=1)) / channels + epsilon)
    normed = (gated * inv_rms[:, None] * norm_gain).astype(jnp.bfloat16)
    weight_grad = jnp.dot(normed.T, grad_rows, preferred_element_type=jnp.float32)
    grad_normed = jnp.dot(grad_rows, w_out.T, preferred_element_type=jnp.float32)
    norm_grad = lax.optimization_barrier(jnp.sum(grad_normed * gated * inv_rms[:, None], axis=0))
    slope = lax.optimization_barrier(jnp.sum(gated * norm_gain * grad_normed, axis=1)) / channels
    cube = inv_rms * inv_rms * inv_rms
    grad_gated = inv_rms[:, None] * norm_gain * grad_normed - gated * (cube * slope)[:, None]
    return (weight_grad, norm_grad) + tuple(pull(grad_gated))

def reference(x_input, z_input, dt_raw, b_rows, c_rows, a_log, skip_gain, dt_bias, norm_gain, w_out, grad_rows, doc_ids):
    x_groups = x_input.reshape(N_DP, SEQ, INNER)
    z_groups = z_input.reshape(N_DP, SEQ, INNER)
    dt_groups = dt_raw.reshape(HEADS, N_DP, SEQ).transpose(1, 0, 2)
    b_groups = b_rows.reshape(N_DP, SEQ, N)
    c_groups = c_rows.reshape(N_DP, SEQ, N)
    grad_groups = grad_rows.reshape(N_DP, SEQ, D)
    id_groups = doc_ids.reshape(N_DP, SEQ)

    def visit(totals, inputs):
        x_one, z_one, dt_one, b_one, c_one, grad_one, ids_one = inputs
        result = group_grads(x_one, z_one, dt_one, b_one, c_one, a_log, skip_gain, dt_bias, norm_gain, w_out, grad_one, ids_one)
        weight_grad, norm_grad, gx, gz, gdt, gb, gc, gal, gsk, gdb = result
        totals = (totals[0] + weight_grad, totals[1] + norm_grad, totals[2] + gal, totals[3] + gsk, totals[4] + gdb)
        return (totals, (gx.astype(jnp.bfloat16), gz.astype(jnp.bfloat16), gdt, gb, gc))
    start = (jnp.zeros((INNER, D), jnp.float32), jnp.zeros((INNER,), jnp.float32), jnp.zeros((HEADS,), jnp.float32), jnp.zeros((HEADS,), jnp.float32), jnp.zeros((HEADS,), jnp.float32))
    totals, stacked = lax.scan(visit, start, (x_groups, z_groups, dt_groups, b_groups, c_groups, grad_groups, id_groups))
    gx, gz, gdt, gb, gc = stacked
    grad_x = gx.reshape(TOKENS, INNER)
    grad_z = gz.reshape(TOKENS, INNER)
    grad_dt = gdt.transpose(1, 0, 2).reshape(HEADS, TOKENS)
    grad_b = gb.reshape(TOKENS, N)
    grad_c = gc.reshape(TOKENS, N)
    return (grad_x, grad_z, grad_dt, grad_b, grad_c, totals[0].astype(jnp.bfloat16), totals[1], totals[2], totals[3], totals[4])
```

```python
import jax
import jax.numpy as jnp
from jax import lax
from jax.experimental import pallas as pl
from jax.experimental.pallas import tpu as pltpu
from jax.sharding import PartitionSpec as P

MESH = pl.DeviceIdType.MESH
HI = lax.Precision.HIGHEST
F32 = jnp.float32
BF16 = jnp.bfloat16
EPS = 1e-05

T = 256
C = 256
HD = 64
NH = 4
N = 128
DW = 2048
NT = 16
NY = 8
CHUNKS = 4
CW = DW // CHUNKS
INNER = C * NT


def nn(a, b, prec=None):
    return lax.dot_general(a, b, (((1,), (0,)), ((), ())), precision=prec, preferred_element_type=F32)


def nt(a, b, prec=None):
    return lax.dot_general(a, b, (((1,), (1,)), ((), ())), precision=prec, preferred_element_type=F32)


def tn(a, b, prec=None):
    return lax.dot_general(a, b, (((0,), (0,)), ((), ())), precision=prec, preferred_element_type=F32)


def kernel(
    x_ref, z_ref, dt_ref, b_ref, c_ref, al_ref, sk_ref, db_ref, gain_ref, w_ref, g_ref, ids_ref,
    gx_ref, gz_ref, gdt_ref, gb_ref, gc_ref, gw_ref, gn_ref, gs_ref,
    bc, gall, st1, st2, wk, r1, s2, r2, s3, r3, dbc, dbr, pk, p1, p2, p2r, p3, p3r,
    rw, pr, mb, tge, xt, xtb, silt, dst, yt, gt, ks, hs, qs, ws, dxt, nrm, mx,
    bc_s, bc_r, g_s, g_r, st1_s, st1_r, st2_s, st2_r, c_s, c_r, x_s, x_r, z_s, z_r,
    az_s, az_r, ax_s, ax_r, ac_s, ac_r, db_s, db_r, p_s, p_r,
):
    dp = lax.axis_index("dp")
    me = lax.axis_index("tensor")
    zl, xi, core = dp // 8, (dp // 2) % 4, dp % 2
    y, zh = me // 2, me % 2

    def at_x(o):
        return zl * 8 + ((xi + o) % 4) * 2 + core

    def at_z(o):
        return ((zl + o) % 4) * 8 + xi * 2 + core

    other_core = zl * 8 + xi * 2 + (1 - core)
    dp_peers = [other_core] + [at_x(o) for o in (1, 2, 3)] + [at_z(o) for o in (1, 2, 3)]

    barrier = pltpu.get_barrier_semaphore()
    for o in range(1, NT):
        pl.semaphore_signal(barrier, inc=1, device_id=(dp, (me + o) % NT), device_id_type=MESH)
    for peer in dp_peers:
        pl.semaphore_signal(barrier, inc=1, device_id=(peer, me), device_id_type=MESH)

    started = []

    def send(src, dst, ss, rs, dev):
        copy = pltpu.make_async_remote_copy(
            src_ref=src, dst_ref=dst, send_sem=ss, recv_sem=rs, device_id=dev, device_id_type=MESH
        )
        copy.start()
        started.append(copy)
        return copy

    def rows(i, n):
        return pl.ds(pl.multiple_of(i * n, n), n)

    bc[rows(me, 16), 0:N] = b_ref[...]
    bc[rows(me, 16), N:2 * N] = c_ref[...]
    gall[rows(me, 16), :] = g_ref[...]

    pl.semaphore_wait(barrier, NT - 1 + len(dp_peers))

    bc_copies = []
    for o in range(1, NT):
        mine = bc.at[rows(me, 16), :]
        bc_copies.append(send(mine, mine, bc_s.at[o - 1], bc_r.at[o - 1], (dp, (me + o) % NT)))

    def piece(slot):
        return gall.at[rows(slot, 16), :]

    ring = {}

    def hop(direction, kind, k):
        ysrc = (y - direction * k + NY) % NY
        slot = ysrc * 2 + (zh if kind == 0 else 1 - zh)
        to = ((y + direction + NY) % NY) * 2 + zh
        i = 1 + ((0 if direction > 0 else 1) * 2 + kind) * 4 + k
        ring[direction, kind, k + 1] = send(piece(slot), piece(slot), g_s.at[i], g_r.at[i], (dp, to))

    zcopy = send(piece(me), piece(me), g_s.at[0], g_r.at[0], (dp, y * 2 + 1 - zh))
    hop(1, 0, 0)
    hop(-1, 0, 0)

    def last_hop(direction, kind):
        return 4 if (direction > 0) == (kind == 0) else 3

    def ring_partner():
        zcopy.wait_recv()
        hop(1, 1, 0)
        hop(-1, 1, 0)

    def ring_level(k):
        for kind in (0, 1):
            for direction in (1, -1):
                if k <= last_hop(direction, kind):
                    ring[direction, kind, k].wait_recv()
                    if k < last_hop(direction, kind):
                        hop(direction, kind, k)

    hrow = lax.broadcasted_iota(jnp.int32, (NH, T), 0)

    def per_head(ref):
        v = jnp.full((NH, T), ref[0], F32)
        for h in range(1, NH):
            v = jnp.where(hrow == h, ref[h], v)
        return v

    pre = dt_ref[...] + per_head(db_ref)
    step = jnp.maximum(pre, 0.0) + jnp.log1p(jnp.exp(-jnp.abs(pre)))
    sig = 1.0 / (1.0 + jnp.exp(-pre))
    ea = jnp.exp(per_head(al_ref))
    ld = -ea * step
    rw[...] = jnp.zeros_like(rw)
    rw[0:NH, :] = step
    rw[4:5, :] = ids_ref[...].astype(F32)
    rw[5:6, :] = gain_ref[...]
    rw[8:8 + NH, :] = ld
    ri = lax.broadcasted_iota(jnp.int32, (T, T), 0)
    ci = lax.broadcasted_iota(jnp.int32, (T, T), 1)
    tril = jnp.where(ri >= ci, 1.0, 0.0)
    eye = jnp.where(ri == ci, 1.0, 0.0)
    tge[...] = tril.astype(BF16)
    cols = nt(eye, rw[0:8, :], HI)
    cumc = nt(tril, rw[8:16, :], HI)
    cumr = nt(rw[8:16, :], tril, HI)
    idr = rw[4:5, :]
    mb[...] = jnp.where((ri <= ci) & (cols[:, 4:5] == idr), 0.0, -1e30)
    gain_col = cols[:, 5:6]

    ring_partner()

    xv = x_ref[...].astype(F32).T
    xt[...] = xv
    xtb[...] = xv.astype(BF16)
    zv = z_ref[...].astype(F32).T
    sg = 1.0 / (1.0 + jnp.exp(-zv))
    silt[...] = zv * sg
    dst[...] = sg * (1.0 + zv * (1.0 - sg))

    ks[...] = jnp.zeros_like(ks)
    hs[...] = jnp.zeros_like(hs)

    for copy in bc_copies:
        copy.wait_recv()
    ring_level(1)
    ball = bc[:, 0:N]
    call = bc[:, N:2 * N]
    scores = nt(ball, call)
    mx[...] = scores
    for h in range(NH):
        for s0 in range(0, T, 64):
            t0 = 0 if s0 < 128 else 128
            gap = cumr[h:h + 1, t0:] - cumc[s0:s0 + 64, h:h + 1] + mb[s0:s0 + 64, t0:]
            w = jnp.exp(gap) * cols[s0:s0 + 64, h:h + 1]
            hs[h, s0:s0 + 64, t0:] = w.astype(BF16)
            ks[h, s0:s0 + 64, t0:] = (w * mx[s0:s0 + 64, t0:]).astype(BF16)
        c0 = h * HD
        yv = nn(xtb[c0:c0 + HD, :], ks[h]) + sk_ref[h] * xt[c0:c0 + HD, :]
        yt[c0:c0 + HD, :] = yv
        gt[c0:c0 + HD, :] = yv * silt[c0:c0 + HD, :]
        if h == 1:
            ring_level(2)

    def all_stats(st, row, ss, rs):
        st[me, 0:1, :] = row[:, 0:128]
        st[me, 1:2, :] = row[:, 128:256]
        return [
            send(st.at[me], st.at[me], ss.at[o - 1], rs.at[o - 1], (dp, (me + o) % NT))
            for o in range(1, NT)
        ]

    def sum_stats(st, copies):
        for copy in copies:
            copy.wait_recv()
        tot = jnp.sum(st[...], axis=0)
        return jnp.concatenate([tot[0:1, :], tot[1:2, :]], axis=1)

    gated = gt[...]
    stat1 = all_stats(st1, jnp.sum(gated * gated, axis=0, keepdims=True), st1_s, st1_r)
    ring_level(3)
    inv = lax.rsqrt(sum_stats(st1, stat1) / INNER + EPS)
    nrm[...] = (gt[...] * inv * gain_col).astype(BF16)
    ring_level(4)

    core_copies = []
    for k in range(CHUNKS):
        wk[k] = nn(nrm[...], gall[:, k * CW:(k + 1) * CW]).astype(BF16)
        core_copies.append(
            send(wk.at[k, rows(1 - core, 128), :], r1.at[k], c_s.at[k], c_r.at[k], (other_core, me))
        )

    mixed = nt(w_ref[...], gall[...])
    mx[...] = mixed
    stat2 = all_stats(
        st2, jnp.sum(gt[...] * gain_col * mixed, axis=0, keepdims=True), st2_s, st2_r
    )

    x_copies = []

    def stage_x(k):
        core_copies[k].wait_recv()
        s2[k] = (wk[k, rows(core, 128), :].astype(F32) + r1[k].astype(F32)).astype(BF16)
        x_copies.append([
            send(
                s2.at[k, rows((xi + o) % 4, 32), :], r2.at[k, o - 1],
                x_s.at[k * 3 + o - 1], x_r.at[k * 3 + o - 1], (at_x(o), me),
            )
            for o in (1, 2, 3)
        ])

    z_copies = []

    def stage_z(k):
        for copy in x_copies[k]:
            copy.wait_recv()
        tot = s2[k, rows(xi, 32), :].astype(F32)
        for o in range(3):
            tot = tot + r2[k, o].astype(F32)
        tot = tot.astype(BF16)
        for q in range(4):
            s3[k, q] = tot[:, q * 128:(q + 1) * 128]
        z_copies.append([
            send(
                s3.at[k, (zl + o) % 4], r3.at[k, o - 1],
                z_s.at[k * 3 + o - 1], z_r.at[k * 3 + o - 1], (at_z(o), me),
            )
            for o in (1, 2, 3)
        ])

    az_copies, ax_copies, ac_copies = [], [], []

    def gather_z(k):
        for copy in z_copies[k]:
            copy.wait_recv()
        tot = s3[k, zl].astype(F32)
        for o in range(3):
            tot = tot + r3[k, o].astype(F32)
        r0 = rows(core * 4 + xi, 32)
        col = pl.ds(pl.multiple_of(k * CW + zl * 128, 128), 128)
        gw_ref[r0, col] = tot.astype(BF16)
        az_copies.append([
            send(
                gw_ref.at[r0, col], gw_ref.at[r0, col],
                az_s.at[k * 3 + o - 1], az_r.at[k * 3 + o - 1], (at_z(o), me),
            )
            for o in (1, 2, 3)
        ])

    def gather_x(k):
        for copy in az_copies[k]:
            copy.wait_recv()
        block = gw_ref.at[rows(core * 4 + xi, 32), k * CW:(k + 1) * CW]
        ax_copies.append([
            send(block, block, ax_s.at[k * 3 + o - 1], ax_r.at[k * 3 + o - 1], (at_x(o), me))
            for o in (1, 2, 3)
        ])

    def gather_core(k):
        for copy in ax_copies[k]:
            copy.wait_recv()
        block = gw_ref.at[rows(core, 128), k * CW:(k + 1) * CW]
        ac_copies.append(send(block, block, ac_s.at[k], ac_r.at[k], (other_core, me)))

    for k in range(CHUNKS):
        stage_x(k)

    slope = sum_stats(st2, stat2) / INNER
    mixed = mx[...]
    gated = gt[...]
    ng = nt(jnp.ones((8, T), F32), mixed * gated * inv, HI)
    ggt = gain_col * mixed * inv - gated * (inv * inv * inv * slope)
    gz_ref[...] = (ggt * yt[...] * dst[...]).T.astype(BF16)
    yt[...] = ggt * silt[...]

    ws[...] = jnp.zeros_like(ws)
    qs[...] = jnp.zeros_like(qs)
    pr[...] = jnp.zeros_like(pr)
    strict = jnp.where(ri < ci, 1.0, 0.0)

    def back(h):
        c0 = h * HD
        dy = yt[c0:c0 + HD, :]
        xh = xt[c0:c0 + HD, :]
        dyb = dy.astype(BF16)
        for s0, t0 in ((0, 0), (128, 128)):
            dm = tn(xtb[c0:c0 + HD, s0:s0 + 128], dyb[:, t0:])
            qs[s0:s0 + 128, t0:] = (dm * ks[h, s0:s0 + 128, t0:].astype(F32)).astype(BF16)
            ws[s0:s0 + 128, t0:] += dm * hs[h, s0:s0 + 128, t0:].astype(F32)
        top = jnp.sum(nn(qs[0:128, :], tge[...]) * strict[0:128, :], axis=0, keepdims=True)
        low = jnp.sum(
            nn(qs[128:, 128:], tge[128:, 128:]) * strict[128:, 128:], axis=0, keepdims=True
        )
        dld = jnp.concatenate([top[:, 0:128], top[:, 128:] + low], axis=1)
        dxi = nt(dyb, ks[h])
        direct = jnp.sum(xh * dxi, axis=0, keepdims=True) / rw[h:h + 1, :]
        dxt[c0:c0 + HD, :] = dxi + sk_ref[h] * dy
        pr[h:h + 1, :] = jnp.sum(dy * xh, axis=0, keepdims=True)
        pr[4 + h:5 + h, :] = dld
        pr[8 + h:9 + h, :] = direct

    for h in range(NH):
        back(h)
        stage_z(h)

    dld = pr[4:8, :]
    ddt = (pr[8:12, :] - ea * dld) * sig
    gdt_ref[...] = ddt
    pr[4:8, :] = dld * ld
    pr[8:12, :] = ddt

    wb = ws[...].astype(BF16)
    dbc[:, 0:N] = nn(wb, call).astype(BF16)
    dbc[:, N:2 * N] = tn(wb, ball).astype(BF16)
    d_copies = [
        send(
            dbc.at[rows((me + o) % NT, 16), :], dbr.at[o - 1],
            db_s.at[o - 1], db_r.at[o - 1], (dp, (me + o) % NT),
        )
        for o in range(1, NT)
    ]

    small = nt(jnp.ones((8, T), F32), pr[...], HI)
    pk[...] = jnp.zeros_like(pk)
    pk[0:1, :] = ng[0:1, 0:128]
    pk[1:2, :] = ng[0:1, 128:256]
    pk[2:3, 0:16] = small[0:1, :]
    pc = send(pk, p1, p_s.at[0], p_r.at[0], (other_core, me))

    for k in range(CHUNKS):
        gather_z(k)

    pc.wait_recv()
    p2[...] = pk[...] + p1[...]
    px = [
        send(p2, p2r.at[o - 1], p_s.at[o], p_r.at[o], (at_x(o), me)) for o in (1, 2, 3)
    ]

    for k in range(CHUNKS):
        gather_x(k)

    gx_ref[...] = dxt[...].T.astype(BF16)
    for copy in px:
        copy.wait_recv()
    p3[...] = p2[...] + p2r[0] + p2r[1] + p2r[2]
    pz = [
        send(p3, p3r.at[o - 1], p_s.at[o + 3], p_r.at[o + 3], (at_z(o), me)) for o in (1, 2, 3)
    ]

    for copy in d_copies:
        copy.wait_recv()
    tot = dbc[rows(me, 16), :].astype(F32)
    for o in range(NT - 1):
        tot = tot + dbr[o].astype(F32)
    gb_ref[...] = tot[:, 0:N]
    gc_ref[...] = tot[:, N:2 * N]

    for k in range(CHUNKS):
        gather_core(k)

    for copy in pz:
        copy.wait_recv()
    tot = p3[...] + p3r[0] + p3r[1] + p3r[2]
    gn_ref[...] = tot[0:2, :]
    gs_ref[...] = tot[2:3, :]

    for copy in ac_copies:
        copy.wait_recv()
    for copy in started:
        copy.wait_send()


def per_device(x, z, dt, b, c, a_log, skip, bias, gain, w, g, ids):
    vmem = pl.BlockSpec(memory_space=pltpu.VMEM)
    smem = pl.BlockSpec(memory_space=pltpu.SMEM)
    v = pltpu.VMEM
    dma = pltpu.SemaphoreType.DMA
    peers = NT - 1
    scratch = [
        v((T, 2 * N), BF16), v((T, DW), BF16), v((NT, 2, 128), F32), v((NT, 2, 128), F32),
        v((CHUNKS, C, CW), BF16), v((CHUNKS, 128, CW), BF16), v((CHUNKS, 128, CW), BF16),
        v((CHUNKS, 3, 32, CW), BF16), v((CHUNKS, 4, 32, 128), BF16), v((CHUNKS, 3, 32, 128), BF16),
        v((T, 2 * N), BF16), v((peers, 16, 2 * N), BF16),
        v((4, 128), F32), v((4, 128), F32), v((4, 128), F32), v((3, 4, 128), F32),
        v((4, 128), F32), v((3, 4, 128), F32),
        v((16, T), F32), v((16, T), F32), v((T, T), F32), v((T, T), BF16),
        v((C, T), F32), v((C, T), BF16), v((C, T), F32), v((C, T), F32), v((C, T), F32),
        v((C, T), F32), v((NH, T, T), BF16), v((NH, T, T), BF16), v((T, T), BF16),
        v((T, T), F32), v((C, T), F32), v((C, T), BF16), v((C, T), F32),
    ]
    counts = [peers, 17, peers, peers, CHUNKS, 3 * CHUNKS, 3 * CHUNKS, 3 * CHUNKS, 3 * CHUNKS,
              CHUNKS, peers, 7]
    for n in counts:
        scratch += [dma((n,)), dma((n,))]
    out = jax.ShapeDtypeStruct
    gx, gz, gdt, gb, gc, gw, gn, gs = pl.pallas_call(
        kernel,
        out_shape=(
            out((T, C), BF16), out((T, C), BF16), out((NH, T), F32), out((16, N), F32),
            out((16, N), F32), out((C, DW), BF16), out((2, 128), F32), out((1, 128), F32),
        ),
        in_specs=[vmem] * 5 + [smem] * 3 + [vmem] * 4,
        out_specs=(vmem,) * 8,
        scratch_shapes=scratch,
        compiler_params=pltpu.CompilerParams(
            collective_id=0, has_side_effects=True, vmem_limit_bytes=48 * 1024 * 1024
        ),
        cost_estimate=pl.CostEstimate(
            flops=2 * 10**9, bytes_accessed=4 * 2**20, transcendentals=10**6
        ),
    )(x, z, dt, b, c, a_log, skip, bias, gain.reshape(1, C), w, g, ids.reshape(1, T))
    return (
        gx, gz, gdt, gb, gc, gw, gn.reshape(C), gs[0, 4:8], gs[0, 0:4], gs[0, 8:12],
    )


def solution(mesh):
    in_specs = (
        P("dp", "tensor"),
        P("dp", "tensor"),
        P("tensor", "dp"),
        P(("dp", "tensor"), None),
        P(("dp", "tensor"), None),
        P("tensor"),
        P("tensor"),
        P("tensor"),
        P("tensor"),
        P("tensor", None),
        P(("dp", "tensor"), None),
        P("dp"),
    )
    out_specs = (
        P("dp", "tensor"),
        P("dp", "tensor"),
        P("tensor", "dp"),
        P(("dp", "tensor"), None),
        P(("dp", "tensor"), None),
        P("tensor", None),
        P("tensor"),
        P("tensor"),
        P("tensor"),
        P("tensor"),
    )
    return jax.shard_map(
        per_device, mesh=mesh, in_specs=in_specs, out_specs=out_specs, check_vma=False
    )
```

```python
import jax
import jax.numpy as jnp
from jax import lax
from jax.experimental import pallas as pl
from jax.experimental.pallas import tpu as pltpu
from jax.sharding import PartitionSpec as P

MESH = pl.DeviceIdType.MESH
HI = lax.Precision.HIGHEST
F32 = jnp.float32
BF16 = jnp.bfloat16
EPS = 1e-05

T = 256
C = 256
HD = 64
NH = 4
N = 128
DW = 2048
NT = 16
NY = 8
CHUNKS = 4
CW = DW // CHUNKS
ROUTE = ("xz", "xz", "zx", "xz")
ORDER = (0, 1, 2, 3)
INNER = C * NT


def nn(a, b, prec=None):
    return lax.dot_general(a, b, (((1,), (0,)), ((), ())), precision=prec, preferred_element_type=F32)


def nt(a, b, prec=None):
    return lax.dot_general(a, b, (((1,), (1,)), ((), ())), precision=prec, preferred_element_type=F32)


def tn(a, b, prec=None):
    return lax.dot_general(a, b, (((0,), (0,)), ((), ())), precision=prec, preferred_element_type=F32)


def kernel(
    x_hbm, z_hbm, dt_hbm, b_hbm, c_hbm, al_hbm, sk_hbm, db_hbm, gain_hbm, w_hbm, g_hbm, ids_hbm,
    gx_ref, gz_ref, gdt_ref, gb_ref, gc_ref, gw_ref, gn_ref, gal_ref, gsk_ref, gdb_ref,
    bc, gall, st1, st2, wk, r1, s2, r2, s3, r3, dbc, dbr, pk, p1, p2, p3,
    x_ref, z_ref, dt_ref, al_ref, sk_ref, db_ref, gain_ref, w_ref, ids_ref,
    rw, pr, mb, tge, xt, xtb, silt, dst, yt, gt, ks, hs, qs, ws, dxt, nrm, mx,
    in_s, bc_s, bc_r, g_s, g_r, st1_s, st1_r, st2_s, st2_r, c_s, c_r, x_s, x_r, z_s, z_r,
    az_s, az_r, ax_s, ax_r, ac_s, ac_r, db_s, db_r, p_s, p_r,
):
    dp = lax.axis_index("dp")
    me = lax.axis_index("tensor")
    zl, xi, core = dp // 8, (dp // 2) % 4, dp % 2
    y, zh = me // 2, me % 2

    def at_x(o):
        return zl * 8 + ((xi + o) % 4) * 2 + core

    def at_z(o):
        return ((zl + o) % 4) * 8 + xi * 2 + core

    other_core = zl * 8 + xi * 2 + (1 - core)
    dp_peers = [other_core] + [at_x(o) for o in (1, 2, 3)] + [at_z(o) for o in (1, 2, 3)]

    barrier = pltpu.get_barrier_semaphore()
    for o in range(1, NT):
        pl.semaphore_signal(barrier, inc=1, device_id=(dp, (me + o) % NT), device_id_type=MESH)
    for peer in dp_peers:
        pl.semaphore_signal(barrier, inc=1, device_id=(peer, me), device_id_type=MESH)

    def send(src, dst, ss, rs, dev):
        copy = pltpu.make_async_remote_copy(
            src_ref=src, dst_ref=dst, send_sem=ss, recv_sem=rs, device_id=dev, device_id_type=MESH
        )
        copy.start()
        return copy

    def both(ref, ss, rs):
        return pltpu.make_async_remote_copy(
            src_ref=ref, dst_ref=ref, send_sem=ss, recv_sem=rs,
            device_id=(other_core, me), device_id_type=MESH,
        )

    sent = []

    def rows(i, n):
        return pl.ds(pl.multiple_of(i * n, n), n)

    loads = [
        pltpu.make_async_copy(src, dst, in_s.at[i])
        for i, (src, dst) in enumerate([
            (b_hbm, bc.at[rows(me, 16), 0:N]), (c_hbm, bc.at[rows(me, 16), N:2 * N]),
            (g_hbm, gall.at[rows(me, 16), :]), (al_hbm, al_ref), (sk_hbm, sk_ref),
            (db_hbm, db_ref), (dt_hbm, dt_ref), (gain_hbm, gain_ref), (ids_hbm, ids_ref),
            (x_hbm, x_ref), (z_hbm, z_ref), (w_hbm, w_ref),
        ])
    ]
    for load in loads:
        load.start()
    for load in loads[:3]:
        load.wait()

    pl.semaphore_wait(barrier, NT - 1 + len(dp_peers))

    g_copies = {}
    spans = {0: (1, 2, 3, 4, -1, -2, -3), 1: (1, 2, 3, -1, -2, -3, -4)}

    def piece(slot):
        return gall.at[rows(slot, 16), :]

    def push(kind, slot, hop, span):
        i = 1 + kind * 7 + spans[kind].index(span)
        to = ((y + hop + NY) % NY) * 2 + zh
        g_copies[kind, span] = send(piece(slot), piece(slot), g_s.at[0], g_r.at[i], (dp, to))

    def direct(kind, slot):
        for d in (2, -2, 1, -1):
            push(kind, slot, d, d)

    def forward(kind):
        half = zh if kind == 0 else 1 - zh
        for d in (1, -1):
            g_copies[kind, 2 * d].wait_recv()
            slot = ((y - 2 * d + NY) % NY) * 2 + half
            if 4 * d in spans[kind]:
                push(kind, slot, 2 * d, 4 * d)
            push(kind, slot, d, 3 * d)

    partner = y * 2 + 1 - zh
    zcopy = send(piece(me), piece(me), g_s.at[0], g_r.at[0], (dp, partner))
    far = sorted(range(1, NT), key=lambda o: -min(o // 2, NY - o // 2))
    for o in far:
        mine = bc.at[rows(me, 16), :]
        send(mine, mine, bc_s.at[0], bc_r.at[0], (dp, (me + o) % NT))
    bc_all = both(bc.at[0:(NT - 1) * 16, :], bc_s.at[0], bc_r.at[0])
    sent.append(bc_all)

    direct(0, me)
    sent.append(both(gall.at[0:(NT - 1) * 16, :], g_s.at[0], g_r.at[0]))

    for load in loads[3:9]:
        load.wait()
    hrow = lax.broadcasted_iota(jnp.int32, (NH, T), 0)

    def per_head(ref):
        v = jnp.full((NH, T), ref[0], F32)
        for h in range(1, NH):
            v = jnp.where(hrow == h, ref[h], v)
        return v

    pre = dt_ref[...] + per_head(db_ref)
    step = jnp.maximum(pre, 0.0) + jnp.log1p(jnp.exp(-jnp.abs(pre)))
    sig = 1.0 / (1.0 + jnp.exp(-pre))
    ea = jnp.exp(per_head(al_ref))
    ld = -ea * step
    rw[...] = jnp.zeros_like(rw)
    rw[0:NH, :] = step
    rw[4:5, :] = ids_ref[...].astype(F32)
    rw[5:6, :] = gain_ref[...]
    rw[8:8 + NH, :] = ld
    ri = lax.broadcasted_iota(jnp.int32, (T, T), 0)
    ci = lax.broadcasted_iota(jnp.int32, (T, T), 1)
    tril = jnp.where(ri >= ci, 1.0, 0.0)
    eye = jnp.where(ri == ci, 1.0, 0.0)
    tge[...] = tril.astype(BF16)
    cols = nt(eye, rw[0:8, :], HI)
    cumc = nt(tril, rw[8:16, :], HI)
    cumr = nt(rw[8:16, :], tril, HI)
    idr = rw[4:5, :]
    mb[...] = jnp.where((ri <= ci) & (cols[:, 4:5] == idr), 0.0, -1e30)
    gain_col = cols[:, 5:6]

    for load in loads[9:]:
        load.wait()
    xv = x_ref[...].astype(F32).T
    xt[...] = xv
    xtb[...] = xv.astype(BF16)
    zv = z_ref[...].astype(F32).T
    sg = 1.0 / (1.0 + jnp.exp(-zv))
    silt[...] = zv * sg
    dst[...] = sg * (1.0 + zv * (1.0 - sg))

    ks[...] = jnp.zeros_like(ks)
    hs[...] = jnp.zeros_like(hs)

    zcopy.wait_recv()
    direct(1, partner)
    forward(0)
    bc_all.wait_recv()
    ball = bc[:, 0:N]
    call = bc[:, N:2 * N]
    scores = nt(ball, call)
    mx[...] = scores
    for h in range(NH):
        for s0 in range(0, T, 64):
            t0 = 0 if s0 < 128 else 128
            gap = cumr[h:h + 1, t0:] - cumc[s0:s0 + 64, h:h + 1] + mb[s0:s0 + 64, t0:]
            w = jnp.exp(gap) * cols[s0:s0 + 64, h:h + 1]
            hs[h, s0:s0 + 64, t0:] = w.astype(BF16)
            ks[h, s0:s0 + 64, t0:] = (w * mx[s0:s0 + 64, t0:]).astype(BF16)
        c0 = h * HD
        yv = nn(xtb[c0:c0 + HD, :], ks[h]) + sk_ref[h] * xt[c0:c0 + HD, :]
        yt[c0:c0 + HD, :] = yv
        gt[c0:c0 + HD, :] = yv * silt[c0:c0 + HD, :]

    def all_stats(st, row, ss, rs):
        st[me, 0:1, :] = row[:, 0:128]
        st[me, 1:2, :] = row[:, 128:256]
        for o in far:
            send(st.at[me], st.at[me], ss.at[0], rs.at[0], (dp, (me + o) % NT))
        sent.append(both(st.at[0:NT - 1], ss.at[0], rs.at[0]))
        return sent[-1]

    def sum_stats(st, copies):
        copies.wait_recv()
        tot = jnp.sum(st[...], axis=0)
        return jnp.concatenate([tot[0:1, :], tot[1:2, :]], axis=1)

    gated = gt[...]
    stat1 = all_stats(st1, jnp.sum(gated * gated, axis=0, keepdims=True), st1_s, st1_r)

    forward(1)
    for (_, span), copy in g_copies.items():
        if abs(span) != 2:
            copy.wait_recv()
    mixed = nt(w_ref[...], gall[...])
    mx[...] = mixed
    stat2 = all_stats(
        st2, jnp.sum(gt[...] * gain_col * mixed, axis=0, keepdims=True), st2_s, st2_r
    )

    inv = lax.rsqrt(sum_stats(st1, stat1) / INNER + EPS)
    nrm[...] = (gt[...] * inv * gain_col).astype(BF16)

    core_copies = {}
    for k in ORDER:
        wk[k] = nn(nrm[...], gall[:, k * CW:(k + 1) * CW]).astype(BF16)
        core_copies[k] = send(
            wk.at[k, rows(1 - core, 128), :], r1.at[k], c_s.at[0], c_r.at[k], (other_core, me)
        )
    sent.append(both(r1, c_s.at[0], c_r.at[0]))

    axes = {"x": (xi, at_x), "z": (zl, at_z)}
    def stage_x(k):
        core_copies[k].wait_recv()
        s2[k] = (wk[k, rows(core, 128), :].astype(F32) + r1[k].astype(F32)).astype(BF16)
        at, to = axes[ROUTE[k][0]]
        for o in (2, 1, 3):
            send(
                s2.at[k, rows((at + o) % 4, 32), :], r2.at[k, o - 1],
                x_s.at[0], x_r.at[k], (to(o), me),
            )

    def stage_z(k):
        both(r2.at[k], x_s.at[0], x_r.at[k]).wait_recv()
        at, _ = axes[ROUTE[k][0]]
        tot = s2[k, rows(at, 32), :].astype(F32)
        for o in range(3):
            tot = tot + r2[k, o].astype(F32)
        tot = tot.astype(BF16)
        for q in range(4):
            s3[k, q] = tot[:, q * 128:(q + 1) * 128]
        at, to = axes[ROUTE[k][1]]
        for o in (2, 1, 3):
            send(
                s3.at[k, (at + o) % 4], r3.at[k, o - 1], z_s.at[0], z_r.at[k], (to(o), me)
            )

    def gather_z(k):
        both(r3.at[k], z_s.at[0], z_r.at[k]).wait_recv()
        at, to = axes[ROUTE[k][1]]
        tot = s3[k, at].astype(F32)
        for o in range(3):
            tot = tot + r3[k, o].astype(F32)
        r0 = rows(core * 4 + axes[ROUTE[k][0]][0], 32)
        col = pl.ds(pl.multiple_of(k * CW + at * 128, 128), 128)
        gw_ref[r0, col] = tot.astype(BF16)
        for o in (2, 1, 3):
            send(
                gw_ref.at[r0, col], gw_ref.at[r0, col], az_s.at[0], az_r.at[k], (to(o), me)
            )

    def gather_x(k):
        both(r3.at[k], az_s.at[0], az_r.at[k]).wait_recv()
        at, to = axes[ROUTE[k][0]]
        block = gw_ref.at[rows(core * 4 + at, 32), k * CW:(k + 1) * CW]
        for o in (2, 1, 3):
            send(block, block, ax_s.at[0], ax_r.at[k], (to(o), me))

    def gather_core(k):
        both(r2.at[k], ax_s.at[0], ax_r.at[k]).wait_recv()
        block = gw_ref.at[rows(core, 128), k * CW:(k + 1) * CW]
        send(block, block, ac_s.at[0], ac_r.at[k], (other_core, me))

    def gather_end(k):
        both(r1.at[k], ac_s.at[0], ac_r.at[k]).wait_recv()

    sent.extend([
        both(r2, x_s.at[0], x_r.at[0]), both(r3, z_s.at[0], z_r.at[0]),
        both(r3, az_s.at[0], az_r.at[0]), both(r2, ax_s.at[0], ax_r.at[0]),
        both(r1, ac_s.at[0], ac_r.at[0]),
    ])

    for k in ORDER:
        stage_x(k)

    for k in ORDER:
        stage_z(k)
    slope = sum_stats(st2, stat2) / INNER
    mixed = mx[...]
    gated = gt[...]
    ng = nt(jnp.ones((8, T), F32), mixed * gated * inv, HI)
    ggt = gain_col * mixed * inv - gated * (inv * inv * inv * slope)
    gz_ref[...] = (ggt * yt[...] * dst[...]).T.astype(BF16)
    yt[...] = ggt * silt[...]

    ws[...] = jnp.zeros_like(ws)
    qs[...] = jnp.zeros_like(qs)
    pr[...] = jnp.zeros_like(pr)
    strict = jnp.where(ri < ci, 1.0, 0.0)

    def back(h):
        c0 = h * HD
        dy = yt[c0:c0 + HD, :]
        xh = xt[c0:c0 + HD, :]
        dyb = dy.astype(BF16)
        for s0, t0 in ((0, 0), (128, 128)):
            dm = tn(xtb[c0:c0 + HD, s0:s0 + 128], dyb[:, t0:])
            qs[s0:s0 + 128, t0:] = (dm * ks[h, s0:s0 + 128, t0:].astype(F32)).astype(BF16)
            ws[s0:s0 + 128, t0:] += dm * hs[h, s0:s0 + 128, t0:].astype(F32)
        top = jnp.sum(nn(qs[0:128, :], tge[...]) * strict[0:128, :], axis=0, keepdims=True)
        low = jnp.sum(
            nn(qs[128:, 128:], tge[128:, 128:]) * strict[128:, 128:], axis=0, keepdims=True
        )
        dld = jnp.concatenate([top[:, 0:128], top[:, 128:] + low], axis=1)
        dxi = nt(dyb, ks[h])
        direct = jnp.sum(xh * dxi, axis=0, keepdims=True) / rw[h:h + 1, :]
        dxt[c0:c0 + HD, :] = dxi + sk_ref[h] * dy
        pr[h:h + 1, :] = jnp.sum(dy * xh, axis=0, keepdims=True)
        pr[4 + h:5 + h, :] = dld
        pr[8 + h:9 + h, :] = direct

    for h in range(NH):
        back(h)

    dld = pr[4:8, :]
    ddt = (pr[8:12, :] - ea * dld) * sig
    gdt_ref[...] = ddt
    pr[4:8, :] = dld * ld
    pr[8:12, :] = ddt

    wb = ws[...].astype(BF16)
    dbc[:, 0:N] = nn(wb, call).astype(BF16)
    dbc[:, N:2 * N] = tn(wb, ball).astype(BF16)
    for o in far:
        send(
            dbc.at[rows((me + o) % NT, 16), :], dbr.at[o - 1],
            db_s.at[0], db_r.at[0], (dp, (me + o) % NT),
        )
    d_all = both(dbr, db_s.at[0], db_r.at[0])
    sent.append(d_all)

    ones = jnp.ones((8, T), F32)
    pk[...] = jnp.zeros_like(pk)
    pk[0:1, :] = ng[0:1, 0:128]
    pk[1:2, :] = ng[0:1, 128:256]
    for q in range(3):
        pk[2 + q:3 + q, 0:NH] = nt(ones, pr[4 * q:4 * q + 4, :], HI)[0:1, :]
    pc = send(pk, p1, p_s.at[0], p_r.at[0], (other_core, me))

    for k in ORDER:
        gather_z(k)
    pc.wait_recv()
    p2[xi] = pk[...] + p1[...]
    for o in (1, 2, 3):
        send(p2.at[xi], p2.at[xi], p_s.at[1], p_r.at[1], (at_x(o), me))
    px = both(p2.at[0:3], p_s.at[1], p_r.at[1])
    gx_ref[...] = dxt[...].T.astype(BF16)
    for k in ORDER:
        gather_x(k)
    px.wait_recv()
    p3[zl] = p2[0] + p2[1] + p2[2] + p2[3]
    for o in (1, 2, 3):
        send(p3.at[zl], p3.at[zl], p_s.at[2], p_r.at[2], (at_z(o), me))
    pz = both(p3.at[0:3], p_s.at[2], p_r.at[2])
    sent.extend([pc, px, pz])
    d_all.wait_recv()
    tot = dbc[rows(me, 16), :].astype(F32)
    for o in range(NT - 1):
        tot = tot + dbr[o].astype(F32)
    gb_ref[...] = tot[:, 0:N]
    gc_ref[...] = tot[:, N:2 * N]
    for k in ORDER:
        gather_core(k)
    pz.wait_recv()
    tot = p3[0] + p3[1] + p3[2] + p3[3]
    gn_ref[...] = tot[0:2, :]
    gsk_ref[...] = tot[2, 0:NH]
    gal_ref[...] = tot[3, 0:NH]
    gdb_ref[...] = tot[4, 0:NH]
    for k in ORDER:
        gather_end(k)
    for copy in sent:
        copy.wait_send()


def finish(*refs):
    n = (len(refs) - 1) // 2
    copies = [pltpu.make_async_copy(refs[i], refs[n + i], refs[-1].at[i]) for i in range(n)]
    for copy in copies:
        copy.start()
    for copy in copies:
        copy.wait()


def per_device(x, z, dt, b, c, a_log, skip, bias, gain, w, g, ids):
    v = pltpu.VMEM
    dma = pltpu.SemaphoreType.DMA
    peers = NT - 1
    scratch = [
        v((T, 2 * N), BF16), v((T, DW), BF16), v((NT, 2, 128), F32), v((NT, 2, 128), F32),
        v((CHUNKS, C, CW), BF16), v((CHUNKS, 128, CW), BF16), v((CHUNKS, 128, CW), BF16),
        v((CHUNKS, 3, 32, CW), BF16), v((CHUNKS, 4, 32, 128), BF16), v((CHUNKS, 3, 32, 128), BF16),
        v((T, 2 * N), BF16), v((peers, 16, 2 * N), BF16),
        v((8, 128), F32), v((8, 128), F32), v((4, 8, 128), F32), v((4, 8, 128), F32),
        v((T, C), BF16), v((T, C), BF16), v((NH, T), F32), pltpu.SMEM((NH,), F32),
        pltpu.SMEM((NH,), F32), pltpu.SMEM((NH,), F32), v((1, C), F32), v((C, DW), BF16),
        v((1, T), jnp.int32),
        v((16, T), F32), v((16, T), F32), v((T, T), F32), v((T, T), BF16),
        v((C, T), F32), v((C, T), BF16), v((C, T), F32), v((C, T), F32), v((C, T), F32),
        v((C, T), F32), v((NH, T, T), BF16), v((NH, T, T), BF16), v((T, T), BF16),
        v((T, T), F32), v((C, T), F32), v((C, T), BF16), v((C, T), F32),
        dma((12,)),
    ]
    counts = [(1, 1), (1, 17), (1, 1), (1, 1)] + [(1, CHUNKS)] * 6 + [(1, 1), (3, 3)]
    for n in counts:
        scratch += [dma((n[0],)), dma((n[1],))]
    out = jax.ShapeDtypeStruct
    vmem = pl.BlockSpec(memory_space=pltpu.VMEM)
    anywhere = pl.BlockSpec(memory_space=pl.ANY)
    small = out((NH,), F32)
    results = pl.pallas_call(
        kernel,
        out_shape=(
            out((T, C), BF16), out((T, C), BF16), out((NH, T), F32), out((16, N), F32),
            out((16, N), F32), out((C, DW), BF16), out((2, 128), F32), small, small, small,
        ),
        in_specs=[anywhere] * 12,
        out_specs=(vmem,) * 10,
        scratch_shapes=scratch,
        compiler_params=pltpu.CompilerParams(
            collective_id=0, has_side_effects=True, vmem_limit_bytes=56 * 1024 * 1024
        ),
        cost_estimate=pl.CostEstimate(
            flops=2 * 10**9, bytes_accessed=4 * 2**20, transcendentals=10**6
        ),
    )(x, z, dt, b, c, a_log, skip, bias, gain.reshape(1, C), w, g, ids.reshape(1, T))
    results = pl.pallas_call(
        finish,
        out_shape=tuple(out(r.shape, r.dtype) for r in results),
        in_specs=[vmem] * 10,
        out_specs=(anywhere,) * 10,
        scratch_shapes=[dma((10,))],
    )(*results)
    gx, gz, gdt, gb, gc, gw, gn, gal, gsk, gdb = results
    return gx, gz, gdt, gb, gc, gw, gn.reshape(C), gal, gsk, gdb


def solution(mesh):
    in_specs = (
        P("dp", "tensor"),
        P("dp", "tensor"),
        P("tensor", "dp"),
        P(("dp", "tensor"), None),
        P(("dp", "tensor"), None),
        P("tensor"),
        P("tensor"),
        P("tensor"),
        P("tensor"),
        P("tensor", None),
        P(("dp", "tensor"), None),
        P("dp"),
    )
    out_specs = (
        P("dp", "tensor"),
        P("dp", "tensor"),
        P("tensor", "dp"),
        P(("dp", "tensor"), None),
        P(("dp", "tensor"), None),
        P("tensor", None),
        P("tensor"),
        P("tensor"),
        P("tensor"),
        P("tensor"),
    )
    return jax.shard_map(
        per_device, mesh=mesh, in_specs=in_specs, out_specs=out_specs, check_vma=False
    )
```

```python
import jax
import jax.numpy as jnp
from jax import lax
from jax.experimental import pallas as pl
from jax.experimental.pallas import tpu as pltpu
from jax.sharding import PartitionSpec as P

MESH = pl.DeviceIdType.MESH
HI = lax.Precision.HIGHEST
F32 = jnp.float32
BF16 = jnp.bfloat16
EPS = 1e-05

T = 256
C = 256
HD = 64
NH = 4
N = 128
DW = 2048
NT = 16
NY = 8
CHUNKS = 4
CW = DW // CHUNKS
HW = DW // 2
ROUTE = ("xz", "xz", "zx", "xz")
WHOLE = (False, False, True, True)
INNER = C * NT


def nn(a, b, prec=None):
    return lax.dot_general(a, b, (((1,), (0,)), ((), ())), precision=prec, preferred_element_type=F32)


def nt(a, b, prec=None):
    return lax.dot_general(a, b, (((1,), (1,)), ((), ())), precision=prec, preferred_element_type=F32)


def tn(a, b, prec=None):
    return lax.dot_general(a, b, (((0,), (0,)), ((), ())), precision=prec, preferred_element_type=F32)


def kernel(
    x_hbm, z_hbm, dt_hbm, b_hbm, c_hbm, al_hbm, sk_hbm, db_hbm, gain_hbm, w_hbm, g_hbm, ids_hbm,
    gx_ref, gz_ref, gdt_ref, gb_ref, gc_ref, gw_ref, gn_ref, gal_ref, gsk_ref, gdb_ref,
    bc, gall, st1, st2, wk, r1, s2, r2, s3, s4, r3, dbc, dbr, pk, p1, p2, p3,
    x_ref, z_ref, dt_ref, al_ref, sk_ref, db_ref, gain_ref, w_ref, ids_ref,
    rw, pr, mb, tge, xt, xtb, silt, dst, yt, gt, ks, hs, qs, ws, dxt, nrm, mx,
    in_s, bc_s, bc_r, g_s, g_r, st1_s, st1_r, st2_s, st2_r, c_s, c_r, x_s, x_r, z_s, z_r,
    az_s, az_r, ax_s, ax_r, ac_s, ac_r, db_s, db_r, p_s, p_r,
):
    dp = lax.axis_index("dp")
    me = lax.axis_index("tensor")
    zl, xi, core = dp // 8, (dp // 2) % 4, dp % 2
    y, zh = me // 2, me % 2

    def at_x(o):
        return zl * 8 + ((xi + o) % 4) * 2 + core

    def at_z(o):
        return ((zl + o) % 4) * 8 + xi * 2 + core

    other_core = zl * 8 + xi * 2 + (1 - core)
    dp_peers = [other_core] + [at_x(o) for o in (1, 2, 3)] + [at_z(o) for o in (1, 2, 3)]

    barrier = pltpu.get_barrier_semaphore()
    for o in range(1, NT):
        pl.semaphore_signal(barrier, inc=1, device_id=(dp, (me + o) % NT), device_id_type=MESH)
    for peer in dp_peers:
        pl.semaphore_signal(barrier, inc=1, device_id=(peer, me), device_id_type=MESH)

    def send(src, dst, ss, rs, dev):
        copy = pltpu.make_async_remote_copy(
            src_ref=src, dst_ref=dst, send_sem=ss, recv_sem=rs, device_id=dev, device_id_type=MESH
        )
        copy.start()
        return copy

    def both(ref, ss, rs):
        return pltpu.make_async_remote_copy(
            src_ref=ref, dst_ref=ref, send_sem=ss, recv_sem=rs,
            device_id=(other_core, me), device_id_type=MESH,
        )

    sent = []

    def rows(i, n):
        return pl.ds(pl.multiple_of(i * n, n), n)

    loads = [
        pltpu.make_async_copy(src, dst, in_s.at[i])
        for i, (src, dst) in enumerate([
            (b_hbm, bc.at[rows(me, 16), 0:N]), (c_hbm, bc.at[rows(me, 16), N:2 * N]),
            (g_hbm, gall.at[rows(me, 16), :]), (al_hbm, al_ref), (sk_hbm, sk_ref),
            (db_hbm, db_ref), (dt_hbm, dt_ref), (gain_hbm, gain_ref), (ids_hbm, ids_ref),
            (x_hbm, x_ref), (z_hbm, z_ref), (w_hbm, w_ref),
        ])
    ]
    for load in loads:
        load.start()
    for load in loads[:3]:
        load.wait()

    pl.semaphore_wait(barrier, NT - 1 + len(dp_peers))

    g_copies = {}
    z_copies = {}
    spans = {0: (1, 2, 3, 4, -1, -2, -3), 1: (1, 2, 3, -1, -2, -3, -4)}
    partner = y * 2 + 1 - zh

    def piece(slot, part):
        return gall.at[rows(slot, 16), part * HW:(part + 1) * HW]

    def push(part, kind, slot, hop, span):
        i = part * 15 + 1 + kind * 7 + spans[kind].index(span)
        to = ((y + hop + NY) % NY) * 2 + zh
        mine = piece(slot, part)
        g_copies[part, kind, span] = send(mine, mine, g_s.at[part], g_r.at[i], (dp, to))

    def cross(part):
        mine = piece(me, part)
        z_copies[part] = send(mine, mine, g_s.at[part], g_r.at[part * 15], (dp, partner))

    def direct(part, kind):
        if kind:
            z_copies[part].wait_recv()
        for d in (2, -2, 1, -1):
            push(part, kind, partner if kind else me, d, d)

    def forward(part, kind):
        half = zh if kind == 0 else 1 - zh
        for d in (1, -1):
            g_copies[part, kind, 2 * d].wait_recv()
            slot = ((y - 2 * d + NY) % NY) * 2 + half
            if 4 * d in spans[kind]:
                push(part, kind, slot, 2 * d, 4 * d)
            push(part, kind, slot, d, 3 * d)

    def arrived(part):
        for (p, _, span), copy in g_copies.items():
            if p == part and abs(span) != 2:
                copy.wait_recv()

    cross(0)
    far = sorted(range(1, NT), key=lambda o: -min(o // 2, NY - o // 2))
    for o in far:
        mine = bc.at[rows(me, 16), :]
        send(mine, mine, bc_s.at[0], bc_r.at[0], (dp, (me + o) % NT))
    bc_all = both(bc.at[0:(NT - 1) * 16, :], bc_s.at[0], bc_r.at[0])
    sent.append(bc_all)

    direct(0, 0)
    cross(1)
    for part in (0, 1):
        sent.append(both(gall.at[0:(NT - 1) * 16, 0:HW], g_s.at[part], g_r.at[part * 15]))

    for load in loads[3:9]:
        load.wait()
    hrow = lax.broadcasted_iota(jnp.int32, (NH, T), 0)

    def per_head(ref):
        v = jnp.full((NH, T), ref[0], F32)
        for h in range(1, NH):
            v = jnp.where(hrow == h, ref[h], v)
        return v

    pre = dt_ref[...] + per_head(db_ref)
    step = jnp.maximum(pre, 0.0) + jnp.log1p(jnp.exp(-jnp.abs(pre)))
    sig = 1.0 / (1.0 + jnp.exp(-pre))
    ea = jnp.exp(per_head(al_ref))
    ld = -ea * step
    rw[...] = jnp.zeros_like(rw)
    rw[0:NH, :] = step
    rw[4:5, :] = ids_ref[...].astype(F32)
    rw[5:6, :] = gain_ref[...]
    rw[8:8 + NH, :] = ld
    ri = lax.broadcasted_iota(jnp.int32, (T, T), 0)
    ci = lax.broadcasted_iota(jnp.int32, (T, T), 1)
    tril = jnp.where(ri >= ci, 1.0, 0.0)
    eye = jnp.where(ri == ci, 1.0, 0.0)
    tge[...] = tril.astype(BF16)
    cols = nt(eye, rw[0:8, :], HI)
    cumc = nt(tril, rw[8:16, :], HI)
    cumr = nt(rw[8:16, :], tril, HI)
    idr = rw[4:5, :]
    mb[...] = jnp.where((ri <= ci) & (cols[:, 4:5] == idr), 0.0, -1e30)
    gain_col = cols[:, 5:6]

    for load in loads[9:]:
        load.wait()
    xv = x_ref[...].astype(F32).T
    xt[...] = xv
    xtb[...] = xv.astype(BF16)
    zv = z_ref[...].astype(F32).T
    sg = 1.0 / (1.0 + jnp.exp(-zv))
    silt[...] = zv * sg
    dst[...] = sg * (1.0 + zv * (1.0 - sg))

    ks[...] = jnp.zeros_like(ks)
    for h in range(NH):
        for s0 in range(0, T, 64):
            t0 = 0 if s0 < 128 else 128
            gap = cumr[h:h + 1, t0:] - cumc[s0:s0 + 64, h:h + 1] + mb[s0:s0 + 64, t0:]
            hs[h, s0:s0 + 64, t0:] = jnp.exp(gap) * cols[s0:s0 + 64, h:h + 1]

    direct(0, 1)
    forward(0, 0)
    direct(1, 0)
    bc_all.wait_recv()
    ball = bc[:, 0:N]
    call = bc[:, N:2 * N]
    scores = nt(ball, call)
    mx[...] = scores
    for h in range(NH):
        for s0 in range(0, T, 64):
            t0 = 0 if s0 < 128 else 128
            ks[h, s0:s0 + 64, t0:] = (
                hs[h, s0:s0 + 64, t0:] * mx[s0:s0 + 64, t0:]
            ).astype(BF16)
        c0 = h * HD
        yv = nn(xtb[c0:c0 + HD, :], ks[h]) + sk_ref[h] * xt[c0:c0 + HD, :]
        yt[c0:c0 + HD, :] = yv
        gt[c0:c0 + HD, :] = yv * silt[c0:c0 + HD, :]

    def all_stats(st, row, ss, rs):
        st[me, 0:1, :] = row[:, 0:128]
        st[me, 1:2, :] = row[:, 128:256]
        for o in far:
            send(st.at[me], st.at[me], ss.at[0], rs.at[0], (dp, (me + o) % NT))
        sent.append(both(st.at[0:NT - 1], ss.at[0], rs.at[0]))
        return sent[-1]

    def sum_stats(st, copies):
        copies.wait_recv()
        tot = jnp.sum(st[...], axis=0)
        return jnp.concatenate([tot[0:1, :], tot[1:2, :]], axis=1)

    gated = gt[...]
    stat1 = all_stats(st1, jnp.sum(gated * gated, axis=0, keepdims=True), st1_s, st1_r)

    forward(0, 1)
    direct(1, 1)
    forward(1, 0)
    arrived(0)
    mx[...] = nt(w_ref[:, 0:HW], gall[:, 0:HW])
    forward(1, 1)
    inv = lax.rsqrt(sum_stats(st1, stat1) / INNER + EPS)
    nrm[...] = (gt[...] * inv * gain_col).astype(BF16)

    core_copies = {}

    def weight(k):
        wk[k] = nn(nrm[...], gall[:, k * CW:(k + 1) * CW]).astype(BF16)
        core_copies[k] = send(
            wk.at[k, rows(1 - core, 128), :], r1.at[k], c_s.at[0], c_r.at[k], (other_core, me)
        )

    sent.append(both(r1, c_s.at[0], c_r.at[0]))

    axes = {"x": (xi, at_x), "z": (zl, at_z)}
    def stage_x(k):
        core_copies[k].wait_recv()
        s2[k] = (wk[k, rows(core, 128), :].astype(F32) + r1[k].astype(F32)).astype(BF16)
        at, to = axes[ROUTE[k][0]]
        for o in (2, 1, 3):
            send(
                s2.at[k, rows((at + o) % 4, 32), :], r2.at[k, o - 1],
                x_s.at[0], x_r.at[k], (to(o), me),
            )

    def stage_z(k):
        both(r2.at[k], x_s.at[0], x_r.at[k]).wait_recv()
        at, _ = axes[ROUTE[k][0]]
        tot = s2[k, rows(at, 32), :].astype(F32)
        for o in range(3):
            tot = tot + r2[k, o].astype(F32)
        tot = tot.astype(BF16)
        at, to = axes[ROUTE[k][1]]
        if WHOLE[k]:
            mine = s4.at[k, at]
            s4[k, at] = tot
            for o in (2, 1, 3):
                send(mine, mine, z_s.at[k], z_r.at[k], (to(o), me))
            return
        for q in range(4):
            s3[k, q] = tot[:, q * 128:(q + 1) * 128]
        for o in (2, 1, 3):
            send(
                s3.at[k, (at + o) % 4], r3.at[k, o - 1], z_s.at[k], z_r.at[k], (to(o), me)
            )

    def gather_z(k):
        both(s4.at[k, 0:3] if WHOLE[k] else r3.at[k], z_s.at[k], z_r.at[k]).wait_recv()
        if WHOLE[k]:
            tot = s4[k, 0].astype(F32)
            for q in range(1, 4):
                tot = tot + s4[k, q].astype(F32)
            r0 = rows(core * 4 + axes[ROUTE[k][0]][0], 32)
            gw_ref[r0, k * CW:(k + 1) * CW] = tot.astype(BF16)
            gather_x(k)
            return
        at, to = axes[ROUTE[k][1]]
        tot = s3[k, at].astype(F32)
        for o in range(3):
            tot = tot + r3[k, o].astype(F32)
        r0 = rows(core * 4 + axes[ROUTE[k][0]][0], 32)
        col = pl.ds(pl.multiple_of(k * CW + at * 128, 128), 128)
        gw_ref[r0, col] = tot.astype(BF16)
        for o in (2, 1, 3):
            send(
                gw_ref.at[r0, col], gw_ref.at[r0, col], az_s.at[0], az_r.at[k], (to(o), me)
            )

    def gather_x(k):
        if not WHOLE[k]:
            both(r3.at[k], az_s.at[0], az_r.at[k]).wait_recv()
        at, to = axes[ROUTE[k][0]]
        block = gw_ref.at[rows(core * 4 + at, 32), k * CW:(k + 1) * CW]
        for o in (2, 1, 3):
            send(block, block, ax_s.at[0], ax_r.at[k], (to(o), me))

    def gather_core(k):
        both(r2.at[k], ax_s.at[0], ax_r.at[k]).wait_recv()
        block = gw_ref.at[rows(core, 128), k * CW:(k + 1) * CW]
        send(block, block, ac_s.at[0], ac_r.at[k], (other_core, me))

    def gather_end(k):
        both(r1.at[k], ac_s.at[0], ac_r.at[k]).wait_recv()

    sent.extend([
        both(s4.at[k, 0:3] if WHOLE[k] else r3.at[k], z_s.at[k], z_r.at[k]) for k in range(CHUNKS)
    ])
    sent.extend([
        both(r2, x_s.at[0], x_r.at[0]), both(r3.at[0:WHOLE.count(False)], az_s.at[0], az_r.at[0]), both(r2, ax_s.at[0], ax_r.at[0]),
        both(r1, ac_s.at[0], ac_r.at[0]),
    ])

    weight(0)
    weight(1)
    stage_x(0)
    stage_x(1)
    arrived(1)
    weight(2)
    weight(3)
    mx[...] += nt(w_ref[:, HW:], gall[:, HW:])
    stat2 = all_stats(
        st2, jnp.sum(gt[...] * gain_col * mx[...], axis=0, keepdims=True), st2_s, st2_r
    )
    stage_x(2)
    stage_x(3)
    for k in (0, 1, 3, 2):
        stage_z(k)
    gather_z(0)
    gather_z(1)
    slope = sum_stats(st2, stat2) / INNER
    mixed = mx[...]
    gated = gt[...]
    ng = nt(jnp.ones((8, T), F32), mixed * gated * inv, HI)
    ggt = gain_col * mixed * inv - gated * (inv * inv * inv * slope)
    gz_ref[...] = (ggt * yt[...] * dst[...]).T.astype(BF16)
    yt[...] = ggt * silt[...]

    ws[...] = jnp.zeros_like(ws)
    qs[...] = jnp.zeros_like(qs)
    pr[...] = jnp.zeros_like(pr)
    strict = jnp.where(ri < ci, 1.0, 0.0)

    def back(h):
        c0 = h * HD
        dy = yt[c0:c0 + HD, :]
        xh = xt[c0:c0 + HD, :]
        dyb = dy.astype(BF16)
        for s0, t0 in ((0, 0), (128, 128)):
            dm = tn(xtb[c0:c0 + HD, s0:s0 + 128], dyb[:, t0:])
            qs[s0:s0 + 128, t0:] = (dm * ks[h, s0:s0 + 128, t0:].astype(F32)).astype(BF16)
            ws[s0:s0 + 128, t0:] += dm * hs[h, s0:s0 + 128, t0:]
        top = jnp.sum(nn(qs[0:128, :], tge[...]) * strict[0:128, :], axis=0, keepdims=True)
        low = jnp.sum(
            nn(qs[128:, 128:], tge[128:, 128:]) * strict[128:, 128:], axis=0, keepdims=True
        )
        dld = jnp.concatenate([top[:, 0:128], top[:, 128:] + low], axis=1)
        dxi = nt(dyb, ks[h])
        direct = jnp.sum(xh * dxi, axis=0, keepdims=True) / rw[h:h + 1, :]
        dxt[c0:c0 + HD, :] = dxi + sk_ref[h] * dy
        pr[h:h + 1, :] = jnp.sum(dy * xh, axis=0, keepdims=True)
        pr[4 + h:5 + h, :] = dld
        pr[8 + h:9 + h, :] = direct

    for h in range(NH):
        back(h)

    dld = pr[4:8, :]
    ddt = (pr[8:12, :] - ea * dld) * sig
    gdt_ref[...] = ddt
    pr[4:8, :] = dld * ld
    pr[8:12, :] = ddt

    wb = ws[...].astype(BF16)
    dbc[:, 0:N] = nn(wb, call).astype(BF16)
    dbc[:, N:2 * N] = tn(wb, ball).astype(BF16)
    ones = jnp.ones((8, T), F32)
    pk[...] = jnp.zeros_like(pk)
    pk[0:1, :] = ng[0:1, 0:128]
    pk[1:2, :] = ng[0:1, 128:256]
    for q in range(3):
        pk[2 + q:3 + q, 0:NH] = nt(ones, pr[4 * q:4 * q + 4, :], HI)[0:1, :]
    pc = send(pk, p1, p_s.at[0], p_r.at[0], (other_core, me))

    for o in far:
        send(
            dbc.at[rows((me + o) % NT, 16), :], dbr.at[o - 1],
            db_s.at[0], db_r.at[0], (dp, (me + o) % NT),
        )
    d_all = both(dbr, db_s.at[0], db_r.at[0])
    sent.append(d_all)
    gather_z(3)
    gather_z(2)
    pc.wait_recv()
    p2[xi] = pk[...] + p1[...]
    for o in (1, 2, 3):
        send(p2.at[xi], p2.at[xi], p_s.at[1], p_r.at[1], (at_x(o), me))
    px = both(p2.at[0:3], p_s.at[1], p_r.at[1])
    gather_x(0)
    gather_x(1)
    gx_ref[...] = dxt[...].T.astype(BF16)
    px.wait_recv()
    p3[zl] = p2[0] + p2[1] + p2[2] + p2[3]
    for o in (1, 2, 3):
        send(p3.at[zl], p3.at[zl], p_s.at[2], p_r.at[2], (at_z(o), me))
    pz = both(p3.at[0:3], p_s.at[2], p_r.at[2])
    sent.extend([pc, px, pz])
    gather_core(0)
    gather_core(1)
    gather_core(3)
    gather_core(2)
    pz.wait_recv()
    tot = p3[0] + p3[1] + p3[2] + p3[3]
    gn_ref[...] = tot[0:2, :]
    gsk_ref[...] = tot[2, 0:NH]
    gal_ref[...] = tot[3, 0:NH]
    gdb_ref[...] = tot[4, 0:NH]
    for k in range(CHUNKS):
        gather_end(k)
    d_all.wait_recv()
    tot = dbc[rows(me, 16), :].astype(F32)
    for o in range(NT - 1):
        tot = tot + dbr[o].astype(F32)
    gb_ref[...] = tot[:, 0:N]
    gc_ref[...] = tot[:, N:2 * N]
    for copy in sent:
        copy.wait_send()


def finish(*refs):
    n = (len(refs) - 1) // 2
    copies = [pltpu.make_async_copy(refs[i], refs[n + i], refs[-1].at[i]) for i in range(n)]
    for copy in copies:
        copy.start()
    for copy in copies:
        copy.wait()


def per_device(x, z, dt, b, c, a_log, skip, bias, gain, w, g, ids):
    v = pltpu.VMEM
    dma = pltpu.SemaphoreType.DMA
    peers = NT - 1
    scratch = [
        v((T, 2 * N), BF16), v((T, DW), BF16), v((NT, 2, 128), F32), v((NT, 2, 128), F32),
        v((CHUNKS, C, CW), BF16), v((CHUNKS, 128, CW), BF16), v((CHUNKS, 128, CW), BF16),
        v((CHUNKS, 3, 32, CW), BF16), v((CHUNKS, 4, 32, 128), BF16), v((CHUNKS, 4, 32, CW), BF16), v((CHUNKS, 3, 32, 128), BF16),
        v((T, 2 * N), BF16), v((peers, 16, 2 * N), BF16),
        v((8, 128), F32), v((8, 128), F32), v((4, 8, 128), F32), v((4, 8, 128), F32),
        v((T, C), BF16), v((T, C), BF16), v((NH, T), F32), pltpu.SMEM((NH,), F32),
        pltpu.SMEM((NH,), F32), pltpu.SMEM((NH,), F32), v((1, C), F32), v((C, DW), BF16),
        v((1, T), jnp.int32),
        v((16, T), F32), v((16, T), F32), v((T, T), F32), v((T, T), BF16),
        v((C, T), F32), v((C, T), BF16), v((C, T), F32), v((C, T), F32), v((C, T), F32),
        v((C, T), F32), v((NH, T, T), BF16), v((NH, T, T), F32), v((T, T), BF16),
        v((T, T), F32), v((C, T), F32), v((C, T), BF16), v((C, T), F32),
        dma((12,)),
    ]
    counts = [(1, 1), (2, 30), (1, 1), (1, 1)] + [(1, CHUNKS)] * 2 + [(CHUNKS, CHUNKS)] + [(1, CHUNKS)] * 3 + [(1, 1), (3, 3)]
    for n in counts:
        scratch += [dma((n[0],)), dma((n[1],))]
    out = jax.ShapeDtypeStruct
    vmem = pl.BlockSpec(memory_space=pltpu.VMEM)
    anywhere = pl.BlockSpec(memory_space=pl.ANY)
    small = out((NH,), F32)
    results = pl.pallas_call(
        kernel,
        out_shape=(
            out((T, C), BF16), out((T, C), BF16), out((NH, T), F32), out((16, N), F32),
            out((16, N), F32), out((C, DW), BF16), out((2, 128), F32), small, small, small,
        ),
        in_specs=[anywhere] * 12,
        out_specs=(vmem,) * 10,
        scratch_shapes=scratch,
        compiler_params=pltpu.CompilerParams(
            collective_id=0, has_side_effects=True, vmem_limit_bytes=56 * 1024 * 1024
        ),
        cost_estimate=pl.CostEstimate(
            flops=2 * 10**9, bytes_accessed=4 * 2**20, transcendentals=10**6
        ),
    )(x, z, dt, b, c, a_log, skip, bias, gain.reshape(1, C), w, g, ids.reshape(1, T))
    results = pl.pallas_call(
        finish,
        out_shape=tuple(out(r.shape, r.dtype) for r in results),
        in_specs=[vmem] * 10,
        out_specs=(anywhere,) * 10,
        scratch_shapes=[dma((10,))],
    )(*results)
    gx, gz, gdt, gb, gc, gw, gn, gal, gsk, gdb = results
    return gx, gz, gdt, gb, gc, gw, gn.reshape(C), gal, gsk, gdb


def solution(mesh):
    in_specs = (
        P("dp", "tensor"),
        P("dp", "tensor"),
        P("tensor", "dp"),
        P(("dp", "tensor"), None),
        P(("dp", "tensor"), None),
        P("tensor"),
        P("tensor"),
        P("tensor"),
        P("tensor"),
        P("tensor", None),
        P(("dp", "tensor"), None),
        P("dp"),
    )
    out_specs = (
        P("dp", "tensor"),
        P("dp", "tensor"),
        P("tensor", "dp"),
        P(("dp", "tensor"), None),
        P(("dp", "tensor"), None),
        P("tensor", None),
        P("tensor"),
        P("tensor"),
        P("tensor"),
        P("tensor"),
    )
    return jax.shard_map(
        per_device, mesh=mesh, in_specs=in_specs, out_specs=out_specs, check_vma=False
    )
```

```python
import jax
import jax.numpy as jnp
from jax import lax
from jax.experimental import pallas as pl
from jax.experimental.pallas import tpu as pltpu
from jax.sharding import PartitionSpec as P

MESH = pl.DeviceIdType.MESH
HI = lax.Precision.HIGHEST
F32 = jnp.float32
BF16 = jnp.bfloat16
EPS = 1e-05

T = 256
C = 256
HD = 64
NH = 4
N = 128
DW = 2048
NT = 16
NY = 8
CHUNKS = 4
CW = DW // CHUNKS
HW = DW // 2
ROUTE = ("xz", "xz", "zx", "xz")
WHOLE = (False, False, True, True)
INNER = C * NT


def nn(a, b, prec=None):
    return lax.dot_general(a, b, (((1,), (0,)), ((), ())), precision=prec, preferred_element_type=F32)


def nt(a, b, prec=None):
    return lax.dot_general(a, b, (((1,), (1,)), ((), ())), precision=prec, preferred_element_type=F32)


def tn(a, b, prec=None):
    return lax.dot_general(a, b, (((0,), (0,)), ((), ())), precision=prec, preferred_element_type=F32)


def kernel(
    x_hbm, z_hbm, dt_hbm, b_hbm, c_hbm, al_hbm, sk_hbm, db_hbm, gain_hbm, w_hbm, g_hbm, ids_hbm,
    gx_ref, gz_ref, gdt_ref, gb_ref, gc_ref, gw_ref, gn_ref, gal_ref, gsk_ref, gdb_ref,
    bc, gall, st1, st2, wk, r1, s2, r2, s3, s4, r3, dbc, dbr, dbp, dbq, pk, p1, p2, p3,
    x_ref, z_ref, dt_ref, al_ref, sk_ref, db_ref, gain_ref, w_ref, ids_ref,
    rw, pr, mb, tge, xt, xtb, silt, dst, yt, gt, ks, hs, qs, ws, dxt, nrm, mx,
    in_s, bc_s, bc_r, g_s, g_r, st1_s, st1_r, st2_s, st2_r, c_s, c_r, x_s, x_r, z_s, z_r,
    az_s, az_r, ax_s, ax_r, ac_s, ac_r, db_s, db_r, p_s, p_r,
):
    dp = lax.axis_index("dp")
    me = lax.axis_index("tensor")
    zl, xi, core = dp // 8, (dp // 2) % 4, dp % 2
    y, zh = me // 2, me % 2

    def at_x(o):
        return zl * 8 + ((xi + o) % 4) * 2 + core

    def at_z(o):
        return ((zl + o) % 4) * 8 + xi * 2 + core

    other_core = zl * 8 + xi * 2 + (1 - core)
    dp_peers = [other_core] + [at_x(o) for o in (1, 2, 3)] + [at_z(o) for o in (1, 2, 3)]

    far = sorted(range(1, NT), key=lambda o: -min(o // 2, NY - o // 2))
    barrier = pltpu.get_barrier_semaphore()
    for o in far:
        pl.semaphore_signal(barrier, inc=1, device_id=(dp, (me + o) % NT), device_id_type=MESH)
    for peer in dp_peers:
        pl.semaphore_signal(barrier, inc=1, device_id=(peer, me), device_id_type=MESH)

    def send(src, dst, ss, rs, dev):
        copy = pltpu.make_async_remote_copy(
            src_ref=src, dst_ref=dst, send_sem=ss, recv_sem=rs, device_id=dev, device_id_type=MESH
        )
        copy.start()
        return copy

    def both(ref, ss, rs):
        return pltpu.make_async_remote_copy(
            src_ref=ref, dst_ref=ref, send_sem=ss, recv_sem=rs,
            device_id=(other_core, me), device_id_type=MESH,
        )

    sent = []

    def rows(i, n):
        return pl.ds(pl.multiple_of(i * n, n), n)

    loads = [
        pltpu.make_async_copy(src, dst, in_s.at[i])
        for i, (src, dst) in enumerate([
            (b_hbm, bc.at[rows(me, 16), 0:N]), (c_hbm, bc.at[rows(me, 16), N:2 * N]),
            (g_hbm, gall.at[rows(me, 16), :]), (al_hbm, al_ref), (sk_hbm, sk_ref),
            (db_hbm, db_ref), (dt_hbm, dt_ref), (gain_hbm, gain_ref), (ids_hbm, ids_ref),
            (x_hbm, x_ref), (z_hbm, z_ref), (w_hbm, w_ref),
        ])
    ]
    for load in loads:
        load.start()
    for load in loads[:3]:
        load.wait()

    pl.semaphore_wait(barrier, NT - 1 + len(dp_peers))

    g_copies = {}
    z_copies = {}
    spans = {0: (1, 2, 3, 4, -1, -2, -3), 1: (1, 2, 3, -1, -2, -3, -4)}
    partner = y * 2 + 1 - zh

    def piece(slot, part):
        return gall.at[rows(slot, 16), part * HW:(part + 1) * HW]

    def push(part, kind, slot, hop, span):
        i = part * 6 + (2 + kind * 2 + (span > 0) if abs(span) == 2 else 1)
        to = ((y + hop + NY) % NY) * 2 + zh
        mine = piece(slot, part)
        g_copies[part, kind, span] = send(mine, mine, g_s.at[part], g_r.at[i], (dp, to))

    def cross(part):
        mine = piece(me, part)
        z_copies[part] = send(mine, mine, g_s.at[part], g_r.at[part * 6], (dp, partner))

    def direct(part, kind):
        if kind:
            z_copies[part].wait_recv()
        for d in (2, -2, 1, -1):
            push(part, kind, partner if kind else me, d, d)

    def forward(part, kind):
        half = zh if kind == 0 else 1 - zh
        for d in (1, -1):
            g_copies[part, kind, 2 * d].wait_recv()
            slot = ((y - 2 * d + NY) % NY) * 2 + half
            if 4 * d in spans[kind]:
                push(part, kind, slot, 2 * d, 4 * d)
            push(part, kind, slot, d, 3 * d)

    def arrived(part):
        rest = gall.at[0:10 * 16, part * HW:(part + 1) * HW]
        both(rest, g_s.at[part], g_r.at[part * 6 + 1]).wait_recv()

    cross(0)
    for o in far:
        mine = bc.at[rows(me, 16), :]
        send(mine, mine, bc_s.at[0], bc_r.at[0], (dp, (me + o) % NT))
    bc_all = both(bc.at[0:(NT - 1) * 16, :], bc_s.at[0], bc_r.at[0])
    sent.append(bc_all)

    direct(0, 0)
    cross(1)
    for part in (0, 1):
        sent.append(both(gall.at[0:(NT - 1) * 16, 0:HW], g_s.at[part], g_r.at[part * 6]))

    for load in loads[3:9]:
        load.wait()
    hrow = lax.broadcasted_iota(jnp.int32, (NH, T), 0)

    def per_head(ref):
        v = jnp.full((NH, T), ref[0], F32)
        for h in range(1, NH):
            v = jnp.where(hrow == h, ref[h], v)
        return v

    pre = dt_ref[...] + per_head(db_ref)
    step = jnp.maximum(pre, 0.0) + jnp.log1p(jnp.exp(-jnp.abs(pre)))
    sig = 1.0 / (1.0 + jnp.exp(-pre))
    ea = jnp.exp(per_head(al_ref))
    ld = -ea * step
    rw[...] = jnp.zeros_like(rw)
    rw[0:NH, :] = step
    rw[4:5, :] = ids_ref[...].astype(F32)
    rw[5:6, :] = gain_ref[...]
    rw[8:8 + NH, :] = ld
    ri = lax.broadcasted_iota(jnp.int32, (T, T), 0)
    ci = lax.broadcasted_iota(jnp.int32, (T, T), 1)
    tril = jnp.where(ri >= ci, 1.0, 0.0)
    eye = jnp.where(ri == ci, 1.0, 0.0)
    tge[...] = tril.astype(BF16)
    cols = nt(eye, rw[0:8, :], HI)
    cumc = nt(tril, rw[8:16, :], HI)
    cumr = nt(rw[8:16, :], tril, HI)
    idr = rw[4:5, :]
    mb[...] = jnp.where((ri <= ci) & (cols[:, 4:5] == idr), 0.0, -1e30)
    gain_col = cols[:, 5:6]

    for load in loads[9:]:
        load.wait()
    xv = x_ref[...].astype(F32).T
    xt[...] = xv
    xtb[...] = xv.astype(BF16)
    zv = z_ref[...].astype(F32).T
    sg = 1.0 / (1.0 + jnp.exp(-zv))
    silt[...] = zv * sg
    dst[...] = sg * (1.0 + zv * (1.0 - sg))

    ks[...] = jnp.zeros_like(ks)
    for h in range(NH):
        for s0 in range(0, T, 64):
            t0 = 0 if s0 < 128 else 128
            gap = cumr[h:h + 1, t0:] - cumc[s0:s0 + 64, h:h + 1] + mb[s0:s0 + 64, t0:]
            hs[h, s0:s0 + 64, t0:] = jnp.exp(gap) * cols[s0:s0 + 64, h:h + 1]

    direct(0, 1)
    forward(0, 0)
    direct(1, 0)
    bc_all.wait_recv()
    ball = bc[:, 0:N]
    call = bc[:, N:2 * N]
    scores = nt(ball, call)
    mx[...] = scores
    for h in range(NH):
        for s0 in range(0, T, 64):
            t0 = 0 if s0 < 128 else 128
            ks[h, s0:s0 + 64, t0:] = (
                hs[h, s0:s0 + 64, t0:] * mx[s0:s0 + 64, t0:]
            ).astype(BF16)
        c0 = h * HD
        yv = nn(xtb[c0:c0 + HD, :], ks[h]) + sk_ref[h] * xt[c0:c0 + HD, :]
        yt[c0:c0 + HD, :] = yv
        gt[c0:c0 + HD, :] = yv * silt[c0:c0 + HD, :]

    def all_stats(st, row, ss, rs):
        st[me, 0:1, :] = row[:, 0:128]
        st[me, 1:2, :] = row[:, 128:256]
        for o in far:
            send(st.at[me], st.at[me], ss.at[0], rs.at[0], (dp, (me + o) % NT))
        sent.append(both(st.at[0:NT - 1], ss.at[0], rs.at[0]))
        return sent[-1]

    def sum_stats(st, copies):
        copies.wait_recv()
        tot = jnp.sum(st[...], axis=0)
        return jnp.concatenate([tot[0:1, :], tot[1:2, :]], axis=1)

    gated = gt[...]
    stat1 = all_stats(st1, jnp.sum(gated * gated, axis=0, keepdims=True), st1_s, st1_r)

    forward(0, 1)
    direct(1, 1)
    forward(1, 0)
    arrived(0)
    mx[...] = nt(w_ref[:, 0:HW], gall[:, 0:HW])
    forward(1, 1)
    inv = lax.rsqrt(sum_stats(st1, stat1) / INNER + EPS)
    nrm[...] = (gt[...] * inv * gain_col).astype(BF16)

    core_copies = {}

    def weight(k):
        wk[k] = nn(nrm[...], gall[:, k * CW:(k + 1) * CW]).astype(BF16)
        core_copies[k] = send(
            wk.at[k, rows(1 - core, 128), :], r1.at[k], c_s.at[0], c_r.at[k], (other_core, me)
        )

    sent.append(both(r1, c_s.at[0], c_r.at[0]))

    axes = {"x": (xi, at_x), "z": (zl, at_z)}
    def stage_x(k):
        core_copies[k].wait_recv()
        s2[k] = (wk[k, rows(core, 128), :].astype(F32) + r1[k].astype(F32)).astype(BF16)
        at, to = axes[ROUTE[k][0]]
        for o in (2, 1, 3):
            send(
                s2.at[k, rows((at + o) % 4, 32), :], r2.at[k, o - 1],
                x_s.at[0], x_r.at[k], (to(o), me),
            )

    def stage_z(k):
        both(r2.at[k], x_s.at[0], x_r.at[k]).wait_recv()
        at, _ = axes[ROUTE[k][0]]
        tot = s2[k, rows(at, 32), :].astype(F32)
        for o in range(3):
            tot = tot + r2[k, o].astype(F32)
        tot = tot.astype(BF16)
        at, to = axes[ROUTE[k][1]]
        if WHOLE[k]:
            mine = s4.at[k, at]
            s4[k, at] = tot
            for o in (2, 1, 3):
                send(mine, mine, z_s.at[k], z_r.at[k], (to(o), me))
            return
        for q in range(4):
            s3[k, q] = tot[:, q * 128:(q + 1) * 128]
        for o in (2, 1, 3):
            send(
                s3.at[k, (at + o) % 4], r3.at[k, o - 1], z_s.at[k], z_r.at[k], (to(o), me)
            )

    def gather_z(k):
        both(s4.at[k, 0:3] if WHOLE[k] else r3.at[k], z_s.at[k], z_r.at[k]).wait_recv()
        if WHOLE[k]:
            tot = s4[k, 0].astype(F32)
            for q in range(1, 4):
                tot = tot + s4[k, q].astype(F32)
            r0 = rows(core * 4 + axes[ROUTE[k][0]][0], 32)
            gw_ref[r0, k * CW:(k + 1) * CW] = tot.astype(BF16)
            gather_x(k)
            return
        at, to = axes[ROUTE[k][1]]
        tot = s3[k, at].astype(F32)
        for o in range(3):
            tot = tot + r3[k, o].astype(F32)
        r0 = rows(core * 4 + axes[ROUTE[k][0]][0], 32)
        col = pl.ds(pl.multiple_of(k * CW + at * 128, 128), 128)
        gw_ref[r0, col] = tot.astype(BF16)
        for o in (2, 1, 3):
            send(
                gw_ref.at[r0, col], gw_ref.at[r0, col], az_s.at[0], az_r.at[k], (to(o), me)
            )

    def gather_x(k):
        if not WHOLE[k]:
            both(r3.at[k], az_s.at[0], az_r.at[k]).wait_recv()
        at, to = axes[ROUTE[k][0]]
        block = gw_ref.at[rows(core * 4 + at, 32), k * CW:(k + 1) * CW]
        for o in (2, 1, 3):
            send(block, block, ax_s.at[0], ax_r.at[k], (to(o), me))

    def gather_core(k):
        both(r2.at[k], ax_s.at[0], ax_r.at[k]).wait_recv()
        block = gw_ref.at[rows(core, 128), k * CW:(k + 1) * CW]
        send(block, block, ac_s.at[0], ac_r.at[k], (other_core, me))

    def gather_end(k):
        both(r1.at[k], ac_s.at[0], ac_r.at[k]).wait_recv()

    sent.extend([
        both(s4.at[k, 0:3] if WHOLE[k] else r3.at[k], z_s.at[k], z_r.at[k]) for k in range(CHUNKS)
    ])
    sent.extend([
        both(r2, x_s.at[0], x_r.at[0]), both(r3.at[0:WHOLE.count(False)], az_s.at[0], az_r.at[0]), both(r2, ax_s.at[0], ax_r.at[0]),
        both(r1, ac_s.at[0], ac_r.at[0]),
    ])

    weight(0)
    weight(1)
    stage_x(0)
    stage_x(1)
    arrived(1)
    weight(2)
    weight(3)
    mx[...] += nt(w_ref[:, HW:], gall[:, HW:])
    stat2 = all_stats(
        st2, jnp.sum(gt[...] * gain_col * mx[...], axis=0, keepdims=True), st2_s, st2_r
    )
    stage_x(2)
    stage_x(3)
    for k in (0, 1, 3, 2):
        stage_z(k)
    gather_z(0)
    gather_z(1)
    slope = sum_stats(st2, stat2) / INNER
    mixed = mx[...]
    gated = gt[...]
    ng = nt(jnp.ones((8, T), F32), mixed * gated * inv, HI)
    ggt = gain_col * mixed * inv - gated * (inv * inv * inv * slope)
    gz_ref[...] = (ggt * yt[...] * dst[...]).T.astype(BF16)
    yt[...] = ggt * silt[...]

    ws[...] = jnp.zeros_like(ws)
    qs[...] = jnp.zeros_like(qs)
    pr[...] = jnp.zeros_like(pr)
    strict = jnp.where(ri < ci, 1.0, 0.0)

    def back(h):
        c0 = h * HD
        dy = yt[c0:c0 + HD, :]
        xh = xt[c0:c0 + HD, :]
        dyb = dy.astype(BF16)
        for s0, t0 in ((0, 0), (128, 128)):
            dm = tn(xtb[c0:c0 + HD, s0:s0 + 128], dyb[:, t0:])
            qs[s0:s0 + 128, t0:] = (dm * ks[h, s0:s0 + 128, t0:].astype(F32)).astype(BF16)
            ws[s0:s0 + 128, t0:] += dm * hs[h, s0:s0 + 128, t0:]
        top = jnp.sum(nn(qs[0:128, :], tge[...]) * strict[0:128, :], axis=0, keepdims=True)
        low = jnp.sum(
            nn(qs[128:, 128:], tge[128:, 128:]) * strict[128:, 128:], axis=0, keepdims=True
        )
        dld = jnp.concatenate([top[:, 0:128], top[:, 128:] + low], axis=1)
        dxi = nt(dyb, ks[h])
        direct = jnp.sum(xh * dxi, axis=0, keepdims=True) / rw[h:h + 1, :]
        dxt[c0:c0 + HD, :] = dxi + sk_ref[h] * dy
        pr[h:h + 1, :] = jnp.sum(dy * xh, axis=0, keepdims=True)
        pr[4 + h:5 + h, :] = dld
        pr[8 + h:9 + h, :] = direct

    for h in range(NH):
        back(h)

    dld = pr[4:8, :]
    ddt = (pr[8:12, :] - ea * dld) * sig
    gdt_ref[...] = ddt
    pr[4:8, :] = dld * ld
    pr[8:12, :] = ddt

    ones = jnp.ones((8, T), F32)
    pk[...] = jnp.zeros_like(pk)
    pk[0:1, :] = ng[0:1, 0:128]
    pk[1:2, :] = ng[0:1, 128:256]
    for q in range(3):
        pk[2 + q:3 + q, 0:NH] = nt(ones, pr[4 * q:4 * q + 4, :], HI)[0:1, :]
    pc = send(pk, p1, p_s.at[0], p_r.at[0], (other_core, me))

    wb = ws[...].astype(BF16)
    dbc[:, 0:N] = nn(wb, call).astype(BF16)
    dbc[:, N:2 * N] = tn(wb, ball).astype(BF16)
    for d in (4, 3, 5, 2, 6, 1, 7):
        to = (y + d) % NY
        send(dbc.at[rows(to, 32), :], dbr.at[d - 1], db_s.at[0], db_r.at[0], (dp, to * 2 + zh))
    d_all = both(dbr, db_s.at[0], db_r.at[0])
    sent.append(d_all)
    pc.wait_recv()
    p2[xi] = pk[...] + p1[...]
    for o in (1, 2, 3):
        send(p2.at[xi], p2.at[xi], p_s.at[1], p_r.at[1], (at_x(o), me))
    px = both(p2.at[0:3], p_s.at[1], p_r.at[1])
    gather_z(3)
    gather_z(2)
    gather_x(0)
    gather_x(1)
    gx_ref[...] = dxt[...].T.astype(BF16)
    px.wait_recv()
    p3[zl] = p2[0] + p2[1] + p2[2] + p2[3]
    for o in (1, 2, 3):
        send(p3.at[zl], p3.at[zl], p_s.at[2], p_r.at[2], (at_z(o), me))
    pz = both(p3.at[0:3], p_s.at[2], p_r.at[2])
    sent.extend([pc, px, pz])
    d_all.wait_recv()
    tot = dbc[rows(y, 32), :].astype(F32)
    for o in range(NY - 1):
        tot = tot + dbr[o].astype(F32)
    dbp[0] = tot[0:16, :]
    dbp[1] = tot[16:32, :]
    d_last = send(dbp.at[1 - zh], dbq, db_s.at[1], db_r.at[1], (dp, partner))
    sent.append(d_last)
    gather_core(0)
    gather_core(1)
    gather_core(3)
    gather_core(2)
    pz.wait_recv()
    tot = p3[0] + p3[1] + p3[2] + p3[3]
    gn_ref[...] = tot[0:2, :]
    gsk_ref[...] = tot[2, 0:NH]
    gal_ref[...] = tot[3, 0:NH]
    gdb_ref[...] = tot[4, 0:NH]
    for k in range(CHUNKS):
        gather_end(k)
    d_last.wait_recv()
    tot = dbp[zh] + dbq[...]
    gb_ref[...] = tot[:, 0:N]
    gc_ref[...] = tot[:, N:2 * N]
    for copy in sent:
        copy.wait_send()


def finish(*refs):
    n = (len(refs) - 1) // 2
    copies = [pltpu.make_async_copy(refs[i], refs[n + i], refs[-1].at[i]) for i in range(n)]
    for copy in copies:
        copy.start()
    for copy in copies:
        copy.wait()


def per_device(x, z, dt, b, c, a_log, skip, bias, gain, w, g, ids):
    v = pltpu.VMEM
    dma = pltpu.SemaphoreType.DMA
    scratch = [
        v((T, 2 * N), BF16), v((T, DW), BF16), v((NT, 2, 128), F32), v((NT, 2, 128), F32),
        v((CHUNKS, C, CW), BF16), v((CHUNKS, 128, CW), BF16), v((CHUNKS, 128, CW), BF16),
        v((CHUNKS, 3, 32, CW), BF16), v((CHUNKS, 4, 32, 128), BF16), v((CHUNKS, 4, 32, CW), BF16), v((CHUNKS, 3, 32, 128), BF16),
        v((T, 2 * N), BF16), v((NY - 1, 32, 2 * N), BF16), v((2, 16, 2 * N), F32),
        v((16, 2 * N), F32),
        v((8, 128), F32), v((8, 128), F32), v((4, 8, 128), F32), v((4, 8, 128), F32),
        v((T, C), BF16), v((T, C), BF16), v((NH, T), F32), pltpu.SMEM((NH,), F32),
        pltpu.SMEM((NH,), F32), pltpu.SMEM((NH,), F32), v((1, C), F32), v((C, DW), BF16),
        v((1, T), jnp.int32),
        v((16, T), F32), v((16, T), F32), v((T, T), F32), v((T, T), BF16),
        v((C, T), F32), v((C, T), BF16), v((C, T), F32), v((C, T), F32), v((C, T), F32),
        v((C, T), F32), v((NH, T, T), BF16), v((NH, T, T), F32), v((T, T), BF16),
        v((T, T), F32), v((C, T), F32), v((C, T), BF16), v((C, T), F32),
        dma((12,)),
    ]
    counts = [(1, 1), (2, 12), (1, 1), (1, 1)] + [(1, CHUNKS)] * 2 + [(CHUNKS, CHUNKS)] + [(1, CHUNKS)] * 3 + [(2, 2), (3, 3)]
    for n in counts:
        scratch += [dma((n[0],)), dma((n[1],))]
    out = jax.ShapeDtypeStruct
    vmem = pl.BlockSpec(memory_space=pltpu.VMEM)
    anywhere = pl.BlockSpec(memory_space=pl.ANY)
    small = out((NH,), F32)
    results = pl.pallas_call(
        kernel,
        out_shape=(
            out((T, C), BF16), out((T, C), BF16), out((NH, T), F32), out((16, N), F32),
            out((16, N), F32), out((C, DW), BF16), out((2, 128), F32), small, small, small,
        ),
        in_specs=[anywhere] * 12,
        out_specs=(vmem,) * 10,
        scratch_shapes=scratch,
        compiler_params=pltpu.CompilerParams(
            collective_id=0, has_side_effects=True, vmem_limit_bytes=56 * 1024 * 1024
        ),
        cost_estimate=pl.CostEstimate(
            flops=2 * 10**9, bytes_accessed=4 * 2**20, transcendentals=10**6
        ),
    )(x, z, dt, b, c, a_log, skip, bias, gain.reshape(1, C), w, g, ids.reshape(1, T))
    results = pl.pallas_call(
        finish,
        out_shape=tuple(out(r.shape, r.dtype) for r in results),
        in_specs=[vmem] * 10,
        out_specs=(anywhere,) * 10,
        scratch_shapes=[dma((10,))],
    )(*results)
    gx, gz, gdt, gb, gc, gw, gn, gal, gsk, gdb = results
    return gx, gz, gdt, gb, gc, gw, gn.reshape(C), gal, gsk, gdb


def solution(mesh):
    in_specs = (
        P("dp", "tensor"),
        P("dp", "tensor"),
        P("tensor", "dp"),
        P(("dp", "tensor"), None),
        P(("dp", "tensor"), None),
        P("tensor"),
        P("tensor"),
        P("tensor"),
        P("tensor"),
        P("tensor", None),
        P(("dp", "tensor"), None),
        P("dp"),
    )
    out_specs = (
        P("dp", "tensor"),
        P("dp", "tensor"),
        P("tensor", "dp"),
        P(("dp", "tensor"), None),
        P(("dp", "tensor"), None),
        P("tensor", None),
        P("tensor"),
        P("tensor"),
        P("tensor"),
        P("tensor"),
    )
    return jax.shard_map(
        per_device, mesh=mesh, in_specs=in_specs, out_specs=out_specs, check_vma=False
    )
```

```python
import jax
import jax.numpy as jnp
from jax import lax
from jax.experimental import pallas as pl
from jax.experimental.pallas import tpu as pltpu
from jax.sharding import PartitionSpec as P

MESH = pl.DeviceIdType.MESH
HI = lax.Precision.HIGHEST
F32 = jnp.float32
BF16 = jnp.bfloat16
EPS = 1e-05

T = 256
C = 256
HD = 64
NH = 4
N = 128
DW = 2048
NT = 16
NY = 8
CHUNKS = 4
CW = DW // CHUNKS
HW = DW // 2
ROUTE = ("xz", "xz", "zx", "xz")
WHOLE = (False, False, True, True)
INNER = C * NT


def nn(a, b, prec=None):
    return lax.dot_general(a, b, (((1,), (0,)), ((), ())), precision=prec, preferred_element_type=F32)


def nt(a, b, prec=None):
    return lax.dot_general(a, b, (((1,), (1,)), ((), ())), precision=prec, preferred_element_type=F32)


def tn(a, b, prec=None):
    return lax.dot_general(a, b, (((0,), (0,)), ((), ())), precision=prec, preferred_element_type=F32)


def kernel(
    x_hbm, z_hbm, dt_hbm, b_hbm, c_hbm, al_hbm, sk_hbm, db_hbm, gain_hbm, w_hbm, g_hbm, ids_hbm,
    gx_ref, gz_ref, gdt_ref, gb_ref, gc_ref, gw_ref, gn_ref, gal_ref, gsk_ref, gdb_ref,
    bc, gall, st1, st2, wk, r1, s2, r2, s3, s4, r3, dbc, dbr, dbp, dbq, pk, p1, p2, p3,
    x_ref, z_ref, dt_ref, al_ref, sk_ref, db_ref, gain_ref, w_ref, ids_ref,
    rw, pr, mb, tge, xt, xtb, silt, dst, yt, gt, ks, hs, qs, ws, dxt, nrm, mx,
    in_s, bc_s, bc_r, g_s, g_r, st1_s, st1_r, st2_s, st2_r, c_s, c_r, x_s, x_r, z_s, z_r,
    az_s, az_r, ax_s, ax_r, ac_s, ac_r, db_s, db_r, p_s, p_r,
):
    dp = lax.axis_index("dp")
    me = lax.axis_index("tensor")
    zl, xi, core = dp // 8, (dp // 2) % 4, dp % 2
    y, zh = me // 2, me % 2

    def at_x(o):
        return zl * 8 + ((xi + o) % 4) * 2 + core

    def at_z(o):
        return ((zl + o) % 4) * 8 + xi * 2 + core

    other_core = zl * 8 + xi * 2 + (1 - core)
    dp_peers = [other_core] + [at_x(o) for o in (1, 2, 3)] + [at_z(o) for o in (1, 2, 3)]

    far = sorted(range(1, NT), key=lambda o: -min(o // 2, NY - o // 2))
    barrier = pltpu.get_barrier_semaphore()
    for o in far:
        pl.semaphore_signal(barrier, inc=1, device_id=(dp, (me + o) % NT), device_id_type=MESH)
    for peer in dp_peers:
        pl.semaphore_signal(barrier, inc=1, device_id=(peer, me), device_id_type=MESH)

    def send(src, dst, ss, rs, dev):
        copy = pltpu.make_async_remote_copy(
            src_ref=src, dst_ref=dst, send_sem=ss, recv_sem=rs, device_id=dev, device_id_type=MESH
        )
        copy.start()
        return copy

    def both(ref, ss, rs):
        return pltpu.make_async_remote_copy(
            src_ref=ref, dst_ref=ref, send_sem=ss, recv_sem=rs,
            device_id=(other_core, me), device_id_type=MESH,
        )

    sent = []

    def rows(i, n):
        return pl.ds(pl.multiple_of(i * n, n), n)

    loads = [
        pltpu.make_async_copy(src, dst, in_s.at[i])
        for i, (src, dst) in enumerate([
            (b_hbm, bc.at[rows(me, 16), 0:N]), (c_hbm, bc.at[rows(me, 16), N:2 * N]),
            (g_hbm, gall.at[rows(me, 16), :]), (al_hbm, al_ref), (sk_hbm, sk_ref),
            (db_hbm, db_ref), (dt_hbm, dt_ref), (gain_hbm, gain_ref), (ids_hbm, ids_ref),
            (x_hbm, x_ref), (z_hbm, z_ref), (w_hbm, w_ref),
        ])
    ]
    for load in loads:
        load.start()
    for load in loads[:3]:
        load.wait()

    pl.semaphore_wait(barrier, NT - 1 + len(dp_peers))

    g_copies = {}
    z_copies = {}
    spans = {0: (1, 2, 3, 4, -1, -2, -3), 1: (1, 2, 3, -1, -2, -3, -4)}
    partner = y * 2 + 1 - zh

    def piece(slot, part):
        return gall.at[rows(slot, 16), part * HW:(part + 1) * HW]

    def push(part, kind, slot, hop, span):
        i = part * 6 + (2 + kind * 2 + (span > 0) if abs(span) == 2 else 1)
        to = ((y + hop + NY) % NY) * 2 + zh
        mine = piece(slot, part)
        g_copies[part, kind, span] = send(mine, mine, g_s.at[part], g_r.at[i], (dp, to))

    def cross(part):
        mine = piece(me, part)
        z_copies[part] = send(mine, mine, g_s.at[part], g_r.at[part * 6], (dp, partner))

    def direct(part, kind):
        if kind:
            z_copies[part].wait_recv()
        for d in (2, -2, 1, -1):
            push(part, kind, partner if kind else me, d, d)

    def forward(part, kind):
        half = zh if kind == 0 else 1 - zh
        for d in (1, -1):
            g_copies[part, kind, 2 * d].wait_recv()
            slot = ((y - 2 * d + NY) % NY) * 2 + half
            if 4 * d in spans[kind]:
                push(part, kind, slot, 2 * d, 4 * d)
            push(part, kind, slot, d, 3 * d)

    def arrived(part):
        rest = gall.at[0:10 * 16, part * HW:(part + 1) * HW]
        both(rest, g_s.at[part], g_r.at[part * 6 + 1]).wait_recv()

    cross(0)
    for o in far:
        mine = bc.at[rows(me, 16), :]
        send(mine, mine, bc_s.at[0], bc_r.at[0], (dp, (me + o) % NT))
    bc_all = both(bc.at[0:(NT - 1) * 16, :], bc_s.at[0], bc_r.at[0])
    sent.append(bc_all)

    direct(0, 0)
    cross(1)
    for part in (0, 1):
        sent.append(both(gall.at[0:(NT - 1) * 16, 0:HW], g_s.at[part], g_r.at[part * 6]))

    for load in loads[3:9]:
        load.wait()
    hrow = lax.broadcasted_iota(jnp.int32, (NH, T), 0)

    def per_head(ref):
        v = jnp.full((NH, T), ref[0], F32)
        for h in range(1, NH):
            v = jnp.where(hrow == h, ref[h], v)
        return v

    pre = dt_ref[...] + per_head(db_ref)
    step = jnp.maximum(pre, 0.0) + jnp.log1p(jnp.exp(-jnp.abs(pre)))
    sig = 1.0 / (1.0 + jnp.exp(-pre))
    ea = jnp.exp(per_head(al_ref))
    ld = -ea * step
    rw[...] = jnp.zeros_like(rw)
    rw[0:NH, :] = step
    rw[4:5, :] = ids_ref[...].astype(F32)
    rw[5:6, :] = gain_ref[...]
    rw[8:8 + NH, :] = ld
    ri = lax.broadcasted_iota(jnp.int32, (T, T), 0)
    ci = lax.broadcasted_iota(jnp.int32, (T, T), 1)
    tril = jnp.where(ri >= ci, 1.0, 0.0)
    eye = jnp.where(ri == ci, 1.0, 0.0)
    tge[...] = tril.astype(BF16)
    cols = nt(eye, rw[0:8, :], HI)
    cumc = nt(tril, rw[8:16, :], HI)
    cumr = nt(rw[8:16, :], tril, HI)
    idr = rw[4:5, :]
    mb[...] = jnp.where((ri <= ci) & (cols[:, 4:5] == idr), 0.0, -1e30)
    gain_col = cols[:, 5:6]

    for load in loads[9:]:
        load.wait()
    xv = x_ref[...].astype(F32).T
    xt[...] = xv
    xtb[...] = xv.astype(BF16)
    zv = z_ref[...].astype(F32).T
    sg = 1.0 / (1.0 + jnp.exp(-zv))
    silt[...] = zv * sg
    dst[...] = sg * (1.0 + zv * (1.0 - sg))

    ks[...] = jnp.zeros_like(ks)
    for h in range(NH):
        for s0 in range(0, T, 64):
            t0 = 0 if s0 < 128 else 128
            gap = cumr[h:h + 1, t0:] - cumc[s0:s0 + 64, h:h + 1] + mb[s0:s0 + 64, t0:]
            hs[h, s0:s0 + 64, t0:] = jnp.exp(gap) * cols[s0:s0 + 64, h:h + 1]

    direct(0, 1)
    forward(0, 0)
    direct(1, 0)
    bc_all.wait_recv()
    ball = bc[:, 0:N]
    call = bc[:, N:2 * N]
    scores = nt(ball, call)
    mx[...] = scores
    for h in range(NH):
        for s0 in range(0, T, 64):
            t0 = 0 if s0 < 128 else 128
            ks[h, s0:s0 + 64, t0:] = (
                hs[h, s0:s0 + 64, t0:] * mx[s0:s0 + 64, t0:]
            ).astype(BF16)
        c0 = h * HD
        yv = nn(xtb[c0:c0 + HD, :], ks[h]) + sk_ref[h] * xt[c0:c0 + HD, :]
        yt[c0:c0 + HD, :] = yv
        gt[c0:c0 + HD, :] = yv * silt[c0:c0 + HD, :]

    def all_stats(st, row, ss, rs):
        st[me, 0:1, :] = row[:, 0:128]
        st[me, 1:2, :] = row[:, 128:256]
        for o in far:
            send(st.at[me], st.at[me], ss.at[0], rs.at[0], (dp, (me + o) % NT))
        sent.append(both(st.at[0:NT - 1], ss.at[0], rs.at[0]))
        return sent[-1]

    def sum_stats(st, copies):
        copies.wait_recv()
        tot = jnp.sum(st[...], axis=0)
        return jnp.concatenate([tot[0:1, :], tot[1:2, :]], axis=1)

    gated = gt[...]
    stat1 = all_stats(st1, jnp.sum(gated * gated, axis=0, keepdims=True), st1_s, st1_r)

    forward(0, 1)
    direct(1, 1)
    forward(1, 0)
    arrived(0)
    mx[...] = nt(w_ref[:, 0:HW], gall[:, 0:HW])
    forward(1, 1)
    inv = lax.rsqrt(sum_stats(st1, stat1) / INNER + EPS)
    nrm[...] = (gt[...] * inv * gain_col).astype(BF16)

    core_copies = {}

    def weight(k):
        wk[k] = nn(nrm[...], gall[:, k * CW:(k + 1) * CW]).astype(BF16)
        core_copies[k] = send(
            wk.at[k, rows(1 - core, 128), :], r1.at[k], c_s.at[0], c_r.at[k], (other_core, me)
        )

    sent.append(both(r1, c_s.at[0], c_r.at[0]))

    axes = {"x": (xi, at_x), "z": (zl, at_z)}
    def stage_x(k):
        core_copies[k].wait_recv()
        s2[k] = (wk[k, rows(core, 128), :].astype(F32) + r1[k].astype(F32)).astype(BF16)
        at, to = axes[ROUTE[k][0]]
        for o in (2, 1, 3):
            send(
                s2.at[k, rows((at + o) % 4, 32), :], r2.at[k, o - 1],
                x_s.at[0], x_r.at[k], (to(o), me),
            )

    def stage_z(k):
        both(r2.at[k], x_s.at[0], x_r.at[k]).wait_recv()
        at, _ = axes[ROUTE[k][0]]
        tot = s2[k, rows(at, 32), :].astype(F32)
        for o in range(3):
            tot = tot + r2[k, o].astype(F32)
        tot = tot.astype(BF16)
        at, to = axes[ROUTE[k][1]]
        if WHOLE[k]:
            mine = s4.at[k, at]
            s4[k, at] = tot
            for o in (2, 1, 3):
                send(mine, mine, z_s.at[k], z_r.at[k], (to(o), me))
            return
        for q in range(4):
            s3[k, q] = tot[:, q * 128:(q + 1) * 128]
        for o in (2, 1, 3):
            send(
                s3.at[k, (at + o) % 4], r3.at[k, o - 1], z_s.at[k], z_r.at[k], (to(o), me)
            )

    def gather_z(k):
        both(s4.at[k, 0:3] if WHOLE[k] else r3.at[k], z_s.at[k], z_r.at[k]).wait_recv()
        if WHOLE[k]:
            tot = s4[k, 0].astype(F32)
            for q in range(1, 4):
                tot = tot + s4[k, q].astype(F32)
            r0 = rows(core * 4 + axes[ROUTE[k][0]][0], 32)
            gw_ref[r0, k * CW:(k + 1) * CW] = tot.astype(BF16)
            gather_x(k)
            return
        at, to = axes[ROUTE[k][1]]
        tot = s3[k, at].astype(F32)
        for o in range(3):
            tot = tot + r3[k, o].astype(F32)
        r0 = rows(core * 4 + axes[ROUTE[k][0]][0], 32)
        col = pl.ds(pl.multiple_of(k * CW + at * 128, 128), 128)
        gw_ref[r0, col] = tot.astype(BF16)
        for o in (2, 1, 3):
            send(
                gw_ref.at[r0, col], gw_ref.at[r0, col], az_s.at[0], az_r.at[k], (to(o), me)
            )

    def gather_x(k):
        if not WHOLE[k]:
            both(r3.at[k], az_s.at[0], az_r.at[k]).wait_recv()
        at, to = axes[ROUTE[k][0]]
        block = gw_ref.at[rows(core * 4 + at, 32), k * CW:(k + 1) * CW]
        for o in (2, 1, 3):
            send(block, block, ax_s.at[0], ax_r.at[k], (to(o), me))

    def gather_core(k):
        both(r2.at[k], ax_s.at[0], ax_r.at[k]).wait_recv()
        block = gw_ref.at[rows(core, 128), k * CW:(k + 1) * CW]
        send(block, block, ac_s.at[0], ac_r.at[k], (other_core, me))

    def gather_end(k):
        both(r1.at[k], ac_s.at[0], ac_r.at[k]).wait_recv()

    sent.extend([
        both(s4.at[k, 0:3] if WHOLE[k] else r3.at[k], z_s.at[k], z_r.at[k]) for k in range(CHUNKS)
    ])
    sent.extend([
        both(r2, x_s.at[0], x_r.at[0]), both(r3.at[0:WHOLE.count(False)], az_s.at[0], az_r.at[0]), both(r2, ax_s.at[0], ax_r.at[0]),
        both(r1, ac_s.at[0], ac_r.at[0]),
    ])

    weight(0)
    weight(1)
    stage_x(0)
    stage_x(1)
    arrived(1)
    weight(2)
    weight(3)
    mx[...] += nt(w_ref[:, HW:], gall[:, HW:])
    stat2 = all_stats(
        st2, jnp.sum(gt[...] * gain_col * mx[...], axis=0, keepdims=True), st2_s, st2_r
    )
    stage_x(2)
    stage_x(3)
    for k in (0, 1, 3, 2):
        stage_z(k)
    slope = sum_stats(st2, stat2) / INNER
    mixed = mx[...]
    gated = gt[...]
    ng = nt(jnp.ones((8, T), F32), mixed * gated * inv, HI)
    ggt = gain_col * mixed * inv - gated * (inv * inv * inv * slope)
    gz_ref[...] = (ggt * yt[...] * dst[...]).T.astype(BF16)
    yt[...] = ggt * silt[...]

    ws[...] = jnp.zeros_like(ws)
    qs[...] = jnp.zeros_like(qs)
    pr[...] = jnp.zeros_like(pr)
    strict = jnp.where(ri < ci, 1.0, 0.0)

    def back(h):
        c0 = h * HD
        dy = yt[c0:c0 + HD, :]
        xh = xt[c0:c0 + HD, :]
        dyb = dy.astype(BF16)
        for s0, t0 in ((0, 0), (128, 128)):
            dm = tn(xtb[c0:c0 + HD, s0:s0 + 128], dyb[:, t0:])
            qs[s0:s0 + 128, t0:] = (dm * ks[h, s0:s0 + 128, t0:].astype(F32)).astype(BF16)
            ws[s0:s0 + 128, t0:] += dm * hs[h, s0:s0 + 128, t0:]
        top = jnp.sum(nn(qs[0:128, :], tge[...]) * strict[0:128, :], axis=0, keepdims=True)
        low = jnp.sum(
            nn(qs[128:, 128:], tge[128:, 128:]) * strict[128:, 128:], axis=0, keepdims=True
        )
        dld = jnp.concatenate([top[:, 0:128], top[:, 128:] + low], axis=1)
        dxi = nt(dyb, ks[h])
        direct = jnp.sum(xh * dxi, axis=0, keepdims=True) / rw[h:h + 1, :]
        dxt[c0:c0 + HD, :] = dxi + sk_ref[h] * dy
        pr[h:h + 1, :] = jnp.sum(dy * xh, axis=0, keepdims=True)
        pr[4 + h:5 + h, :] = dld
        pr[8 + h:9 + h, :] = direct

    for h in range(NH):
        back(h)

    gather_z(0)
    gather_z(1)
    dld = pr[4:8, :]
    ddt = (pr[8:12, :] - ea * dld) * sig
    gdt_ref[...] = ddt
    pr[4:8, :] = dld * ld
    pr[8:12, :] = ddt

    ones = jnp.ones((8, T), F32)
    pk[...] = jnp.zeros_like(pk)
    pk[0:1, :] = ng[0:1, 0:128]
    pk[1:2, :] = ng[0:1, 128:256]
    for q in range(3):
        pk[2 + q:3 + q, 0:NH] = nt(ones, pr[4 * q:4 * q + 4, :], HI)[0:1, :]
    pc = send(pk, p1, p_s.at[0], p_r.at[0], (other_core, me))

    wb = ws[...].astype(BF16)
    dbc[:, 0:N] = nn(wb, call).astype(BF16)
    dbc[:, N:2 * N] = tn(wb, ball).astype(BF16)
    for d in (4, 3, 5, 2, 6, 1, 7):
        to = (y + d) % NY
        send(dbc.at[rows(to, 32), :], dbr.at[d - 1], db_s.at[0], db_r.at[0], (dp, to * 2 + zh))
    d_all = both(dbr, db_s.at[0], db_r.at[0])
    sent.append(d_all)
    pc.wait_recv()
    p2[xi] = pk[...] + p1[...]
    for o in (1, 2, 3):
        send(p2.at[xi], p2.at[xi], p_s.at[1], p_r.at[1], (at_x(o), me))
    px = both(p2.at[0:3], p_s.at[1], p_r.at[1])
    gather_z(3)
    gather_z(2)
    gather_x(0)
    gather_x(1)
    gx_ref[...] = dxt[...].T.astype(BF16)
    px.wait_recv()
    p3[zl] = p2[0] + p2[1] + p2[2] + p2[3]
    for o in (1, 2, 3):
        send(p3.at[zl], p3.at[zl], p_s.at[2], p_r.at[2], (at_z(o), me))
    pz = both(p3.at[0:3], p_s.at[2], p_r.at[2])
    sent.extend([pc, px, pz])
    d_all.wait_recv()
    tot = dbc[rows(y, 32), :].astype(F32)
    for o in range(NY - 1):
        tot = tot + dbr[o].astype(F32)
    dbp[0] = tot[0:16, :]
    dbp[1] = tot[16:32, :]
    d_last = send(dbp.at[1 - zh], dbq, db_s.at[1], db_r.at[1], (dp, partner))
    sent.append(d_last)
    gather_core(3)
    gather_core(2)
    gather_core(0)
    gather_core(1)
    pz.wait_recv()
    tot = p3[0] + p3[1] + p3[2] + p3[3]
    gn_ref[...] = tot[0:2, :]
    gsk_ref[...] = tot[2, 0:NH]
    gal_ref[...] = tot[3, 0:NH]
    gdb_ref[...] = tot[4, 0:NH]
    d_last.wait_recv()
    tot = dbp[zh] + dbq[...]
    gb_ref[...] = tot[:, 0:N]
    gc_ref[...] = tot[:, N:2 * N]
    for k in range(CHUNKS):
        gather_end(k)
    for copy in sent:
        copy.wait_send()


def finish(*refs):
    n = (len(refs) - 1) // 2
    copies = [pltpu.make_async_copy(refs[i], refs[n + i], refs[-1].at[i]) for i in range(n)]
    for copy in copies:
        copy.start()
    for copy in copies:
        copy.wait()


def per_device(x, z, dt, b, c, a_log, skip, bias, gain, w, g, ids):
    v = pltpu.VMEM
    dma = pltpu.SemaphoreType.DMA
    scratch = [
        v((T, 2 * N), BF16), v((T, DW), BF16), v((NT, 2, 128), F32), v((NT, 2, 128), F32),
        v((CHUNKS, C, CW), BF16), v((CHUNKS, 128, CW), BF16), v((CHUNKS, 128, CW), BF16),
        v((CHUNKS, 3, 32, CW), BF16), v((CHUNKS, 4, 32, 128), BF16), v((CHUNKS, 4, 32, CW), BF16), v((CHUNKS, 3, 32, 128), BF16),
        v((T, 2 * N), BF16), v((NY - 1, 32, 2 * N), BF16), v((2, 16, 2 * N), F32),
        v((16, 2 * N), F32),
        v((8, 128), F32), v((8, 128), F32), v((4, 8, 128), F32), v((4, 8, 128), F32),
        v((T, C), BF16), v((T, C), BF16), v((NH, T), F32), pltpu.SMEM((NH,), F32),
        pltpu.SMEM((NH,), F32), pltpu.SMEM((NH,), F32), v((1, C), F32), v((C, DW), BF16),
        v((1, T), jnp.int32),
        v((16, T), F32), v((16, T), F32), v((T, T), F32), v((T, T), BF16),
        v((C, T), F32), v((C, T), BF16), v((C, T), F32), v((C, T), F32), v((C, T), F32),
        v((C, T), F32), v((NH, T, T), BF16), v((NH, T, T), F32), v((T, T), BF16),
        v((T, T), F32), v((C, T), F32), v((C, T), BF16), v((C, T), F32),
        dma((12,)),
    ]
    counts = [(1, 1), (2, 12), (1, 1), (1, 1)] + [(1, CHUNKS)] * 2 + [(CHUNKS, CHUNKS)] + [(1, CHUNKS)] * 3 + [(2, 2), (3, 3)]
    for n in counts:
        scratch += [dma((n[0],)), dma((n[1],))]
    out = jax.ShapeDtypeStruct
    vmem = pl.BlockSpec(memory_space=pltpu.VMEM)
    anywhere = pl.BlockSpec(memory_space=pl.ANY)
    small = out((NH,), F32)
    results = pl.pallas_call(
        kernel,
        out_shape=(
            out((T, C), BF16), out((T, C), BF16), out((NH, T), F32), out((16, N), F32),
            out((16, N), F32), out((C, DW), BF16), out((2, 128), F32), small, small, small,
        ),
        in_specs=[anywhere] * 12,
        out_specs=(vmem,) * 10,
        scratch_shapes=scratch,
        compiler_params=pltpu.CompilerParams(
            collective_id=0, has_side_effects=True, vmem_limit_bytes=56 * 1024 * 1024
        ),
        cost_estimate=pl.CostEstimate(
            flops=2 * 10**9, bytes_accessed=4 * 2**20, transcendentals=10**6
        ),
    )(x, z, dt, b, c, a_log, skip, bias, gain.reshape(1, C), w, g, ids.reshape(1, T))
    results = pl.pallas_call(
        finish,
        out_shape=tuple(out(r.shape, r.dtype) for r in results),
        in_specs=[vmem] * 10,
        out_specs=(anywhere,) * 10,
        scratch_shapes=[dma((10,))],
    )(*results)
    gx, gz, gdt, gb, gc, gw, gn, gal, gsk, gdb = results
    return gx, gz, gdt, gb, gc, gw, gn.reshape(C), gal, gsk, gdb


def solution(mesh):
    in_specs = (
        P("dp", "tensor"),
        P("dp", "tensor"),
        P("tensor", "dp"),
        P(("dp", "tensor"), None),
        P(("dp", "tensor"), None),
        P("tensor"),
        P("tensor"),
        P("tensor"),
        P("tensor"),
        P("tensor", None),
        P(("dp", "tensor"), None),
        P("dp"),
    )
    out_specs = (
        P("dp", "tensor"),
        P("dp", "tensor"),
        P("tensor", "dp"),
        P(("dp", "tensor"), None),
        P(("dp", "tensor"), None),
        P("tensor", None),
        P("tensor"),
        P("tensor"),
        P("tensor"),
        P("tensor"),
    )
    return jax.shard_map(
        per_device, mesh=mesh, in_specs=in_specs, out_specs=out_specs, check_vma=False
    )
```

```python
import jax
import jax.numpy as jnp
from jax import lax
from jax.experimental import pallas as pl
from jax.experimental.pallas import tpu as pltpu
from jax.sharding import PartitionSpec as P

MESH = pl.DeviceIdType.MESH
HI = lax.Precision.HIGHEST
F32 = jnp.float32
BF16 = jnp.bfloat16
EPS = 1e-05

T = 256
C = 256
HD = 64
NH = 4
N = 128
DW = 2048
NT = 16
NY = 8
CHUNKS = 4
CW = DW // CHUNKS
HW = DW // 2
ROUTE = ("xz", "xz", "zx", "xz")
WHOLE = (False, False, True, True)
INNER = C * NT


def nn(a, b, prec=None):
    return lax.dot_general(a, b, (((1,), (0,)), ((), ())), precision=prec, preferred_element_type=F32)


def nt(a, b, prec=None):
    return lax.dot_general(a, b, (((1,), (1,)), ((), ())), precision=prec, preferred_element_type=F32)


def tn(a, b, prec=None):
    return lax.dot_general(a, b, (((0,), (0,)), ((), ())), precision=prec, preferred_element_type=F32)


def kernel(
    x_hbm, z_hbm, dt_hbm, b_hbm, c_hbm, al_hbm, sk_hbm, db_hbm, gain_hbm, w_hbm, g_hbm, ids_hbm,
    gx_ref, gz_ref, gdt_ref, gb_ref, gc_ref, gw_ref, gn_ref, gal_ref, gsk_ref, gdb_ref,
    bc, gall, st1, st2, wk, r1, s2, r2, s3, s4, r3, dbc, dbr, dbp, dbq, pk, p1, p2, p3,
    x_ref, z_ref, dt_ref, al_ref, sk_ref, db_ref, gain_ref, w_ref, ids_ref,
    rw, pr, mb, tge, xt, xtb, silt, dst, yt, gt, ks, hs, qs, ws, dxt, nrm, mx,
    in_s, bc_s, bc_r, g_s, g_r, st1_s, st1_r, st2_s, st2_r, c_s, c_r, x_s, x_r, z_s, z_r,
    az_s, az_r, ax_s, ax_r, ac_s, ac_r, db_s, db_r, p_s, p_r,
):
    dp = lax.axis_index("dp")
    me = lax.axis_index("tensor")
    zl, xi, core = dp // 8, (dp // 2) % 4, dp % 2
    y, zh = me // 2, me % 2

    def at_x(o):
        return zl * 8 + ((xi + o) % 4) * 2 + core

    def at_z(o):
        return ((zl + o) % 4) * 8 + xi * 2 + core

    other_core = zl * 8 + xi * 2 + (1 - core)
    dp_peers = [other_core] + [at_x(o) for o in (1, 2, 3)] + [at_z(o) for o in (1, 2, 3)]

    far = sorted(range(1, NT), key=lambda o: -min(o // 2, NY - o // 2))
    barrier = pltpu.get_barrier_semaphore()
    for o in far:
        pl.semaphore_signal(barrier, inc=1, device_id=(dp, (me + o) % NT), device_id_type=MESH)
    for peer in dp_peers:
        pl.semaphore_signal(barrier, inc=1, device_id=(peer, me), device_id_type=MESH)

    def send(src, dst, ss, rs, dev):
        copy = pltpu.make_async_remote_copy(
            src_ref=src, dst_ref=dst, send_sem=ss, recv_sem=rs, device_id=dev, device_id_type=MESH
        )
        copy.start()
        return copy

    def both(ref, ss, rs):
        return pltpu.make_async_remote_copy(
            src_ref=ref, dst_ref=ref, send_sem=ss, recv_sem=rs,
            device_id=(other_core, me), device_id_type=MESH,
        )

    sent = []

    def rows(i, n):
        return pl.ds(pl.multiple_of(i * n, n), n)

    loads = [
        pltpu.make_async_copy(src, dst, in_s.at[i])
        for i, (src, dst) in enumerate([
            (b_hbm, bc.at[rows(me, 16), 0:N]), (c_hbm, bc.at[rows(me, 16), N:2 * N]),
            (g_hbm, gall.at[rows(me, 16), :]), (al_hbm, al_ref), (sk_hbm, sk_ref),
            (db_hbm, db_ref), (dt_hbm, dt_ref), (gain_hbm, gain_ref), (ids_hbm, ids_ref),
            (x_hbm, x_ref), (z_hbm, z_ref), (w_hbm, w_ref),
        ])
    ]
    for load in loads:
        load.start()
    for load in loads[:3]:
        load.wait()

    pl.semaphore_wait(barrier, NT - 1 + len(dp_peers))

    g_copies = {}
    z_copies = {}
    spans = {0: (1, 2, 3, 4, -1, -2, -3), 1: (1, 2, 3, -1, -2, -3, -4)}
    partner = y * 2 + 1 - zh

    def piece(slot, part):
        return gall.at[rows(slot, 16), part * HW:(part + 1) * HW]

    def push(part, kind, slot, hop, span):
        i = part * 6 + (2 + kind * 2 + (span > 0) if abs(span) == 2 else 1)
        to = ((y + hop + NY) % NY) * 2 + zh
        mine = piece(slot, part)
        g_copies[part, kind, span] = send(mine, mine, g_s.at[part], g_r.at[i], (dp, to))

    def cross(part):
        mine = piece(me, part)
        z_copies[part] = send(mine, mine, g_s.at[part], g_r.at[part * 6], (dp, partner))

    def direct(part, kind):
        if kind:
            z_copies[part].wait_recv()
        for d in (2, -2, 1, -1):
            push(part, kind, partner if kind else me, d, d)

    def forward(part, kind):
        half = zh if kind == 0 else 1 - zh
        for d in (1, -1):
            g_copies[part, kind, 2 * d].wait_recv()
            slot = ((y - 2 * d + NY) % NY) * 2 + half
            if 4 * d in spans[kind]:
                push(part, kind, slot, 2 * d, 4 * d)
            push(part, kind, slot, d, 3 * d)

    def arrived(part):
        rest = gall.at[0:10 * 16, part * HW:(part + 1) * HW]
        both(rest, g_s.at[part], g_r.at[part * 6 + 1]).wait_recv()

    cross(0)
    for o in far:
        mine = bc.at[rows(me, 16), :]
        send(mine, mine, bc_s.at[0], bc_r.at[0], (dp, (me + o) % NT))
    bc_all = both(bc.at[0:(NT - 1) * 16, :], bc_s.at[0], bc_r.at[0])
    sent.append(bc_all)

    direct(0, 0)
    cross(1)
    for part in (0, 1):
        sent.append(both(gall.at[0:(NT - 1) * 16, 0:HW], g_s.at[part], g_r.at[part * 6]))

    for load in loads[3:9]:
        load.wait()
    hrow = lax.broadcasted_iota(jnp.int32, (NH, T), 0)

    def per_head(ref):
        v = jnp.full((NH, T), ref[0], F32)
        for h in range(1, NH):
            v = jnp.where(hrow == h, ref[h], v)
        return v

    pre = dt_ref[...] + per_head(db_ref)
    step = jnp.maximum(pre, 0.0) + jnp.log1p(jnp.exp(-jnp.abs(pre)))
    sig = 1.0 / (1.0 + jnp.exp(-pre))
    ea = jnp.exp(per_head(al_ref))
    ld = -ea * step
    rw[...] = jnp.zeros_like(rw)
    rw[0:NH, :] = step
    rw[4:5, :] = ids_ref[...].astype(F32)
    rw[5:6, :] = gain_ref[...]
    rw[8:8 + NH, :] = ld
    ri = lax.broadcasted_iota(jnp.int32, (T, T), 0)
    ci = lax.broadcasted_iota(jnp.int32, (T, T), 1)
    tril = jnp.where(ri >= ci, 1.0, 0.0)
    eye = jnp.where(ri == ci, 1.0, 0.0)
    tge[...] = tril.astype(BF16)
    cols = nt(eye, rw[0:8, :], HI)
    cumc = nt(tril, rw[8:16, :], HI)
    cumr = nt(rw[8:16, :], tril, HI)
    idr = rw[4:5, :]
    mb[...] = jnp.where((ri <= ci) & (cols[:, 4:5] == idr), 0.0, -1e30)
    gain_col = cols[:, 5:6]

    for load in loads[9:]:
        load.wait()
    xv = x_ref[...].astype(F32).T
    xt[...] = xv
    xtb[...] = xv.astype(BF16)
    zv = z_ref[...].astype(F32).T
    sg = 1.0 / (1.0 + jnp.exp(-zv))
    silt[...] = zv * sg
    dst[...] = sg * (1.0 + zv * (1.0 - sg))

    ks[...] = jnp.zeros_like(ks)
    for h in range(NH):
        for s0 in range(0, T, 64):
            t0 = 0 if s0 < 128 else 128
            gap = cumr[h:h + 1, t0:] - cumc[s0:s0 + 64, h:h + 1] + mb[s0:s0 + 64, t0:]
            hs[h, s0:s0 + 64, t0:] = jnp.exp(gap) * cols[s0:s0 + 64, h:h + 1]

    direct(0, 1)
    forward(0, 0)
    bc_all.wait_recv()
    ball = bc[:, 0:N]
    call = bc[:, N:2 * N]
    scores = nt(ball, call)
    mx[...] = scores
    for h in range(NH):
        for s0 in range(0, T, 64):
            t0 = 0 if s0 < 128 else 128
            ks[h, s0:s0 + 64, t0:] = (
                hs[h, s0:s0 + 64, t0:] * mx[s0:s0 + 64, t0:]
            ).astype(BF16)
        c0 = h * HD
        yv = nn(xtb[c0:c0 + HD, :], ks[h]) + sk_ref[h] * xt[c0:c0 + HD, :]
        yt[c0:c0 + HD, :] = yv
        gt[c0:c0 + HD, :] = yv * silt[c0:c0 + HD, :]

    def all_stats(st, row, ss, rs):
        st[me, 0:1, :] = row[:, 0:128]
        st[me, 1:2, :] = row[:, 128:256]
        for o in far:
            send(st.at[me], st.at[me], ss.at[0], rs.at[0], (dp, (me + o) % NT))
        sent.append(both(st.at[0:NT - 1], ss.at[0], rs.at[0]))
        return sent[-1]

    def sum_stats(st, copies):
        copies.wait_recv()
        tot = jnp.sum(st[...], axis=0)
        return jnp.concatenate([tot[0:1, :], tot[1:2, :]], axis=1)

    gated = gt[...]
    stat1 = all_stats(st1, jnp.sum(gated * gated, axis=0, keepdims=True), st1_s, st1_r)

    direct(1, 0)
    forward(0, 1)
    direct(1, 1)
    forward(1, 0)
    arrived(0)
    mx[...] = nt(w_ref[:, 0:HW], gall[:, 0:HW])
    forward(1, 1)
    inv = lax.rsqrt(sum_stats(st1, stat1) / INNER + EPS)
    nrm[...] = (gt[...] * inv * gain_col).astype(BF16)

    core_copies = {}

    def weight(k):
        wk[k] = nn(nrm[...], gall[:, k * CW:(k + 1) * CW]).astype(BF16)
        core_copies[k] = send(
            wk.at[k, rows(1 - core, 128), :], r1.at[k], c_s.at[0], c_r.at[k], (other_core, me)
        )

    sent.append(both(r1, c_s.at[0], c_r.at[0]))

    axes = {"x": (xi, at_x), "z": (zl, at_z)}
    def stage_x(k):
        core_copies[k].wait_recv()
        s2[k] = (wk[k, rows(core, 128), :].astype(F32) + r1[k].astype(F32)).astype(BF16)
        at, to = axes[ROUTE[k][0]]
        for o in (2, 1, 3):
            send(
                s2.at[k, rows((at + o) % 4, 32), :], r2.at[k, o - 1],
                x_s.at[0], x_r.at[k], (to(o), me),
            )

    def stage_z(k):
        both(r2.at[k], x_s.at[0], x_r.at[k]).wait_recv()
        at, _ = axes[ROUTE[k][0]]
        tot = s2[k, rows(at, 32), :].astype(F32)
        for o in range(3):
            tot = tot + r2[k, o].astype(F32)
        tot = tot.astype(BF16)
        at, to = axes[ROUTE[k][1]]
        if WHOLE[k]:
            mine = s4.at[k, at]
            s4[k, at] = tot
            for o in (2, 1, 3):
                send(mine, mine, z_s.at[k], z_r.at[k], (to(o), me))
            return
        for q in range(4):
            s3[k, q] = tot[:, q * 128:(q + 1) * 128]
        for o in (2, 1, 3):
            send(
                s3.at[k, (at + o) % 4], r3.at[k, o - 1], z_s.at[k], z_r.at[k], (to(o), me)
            )

    def gather_z(k):
        both(s4.at[k, 0:3] if WHOLE[k] else r3.at[k], z_s.at[k], z_r.at[k]).wait_recv()
        if WHOLE[k]:
            tot = s4[k, 0].astype(F32)
            for q in range(1, 4):
                tot = tot + s4[k, q].astype(F32)
            r0 = rows(core * 4 + axes[ROUTE[k][0]][0], 32)
            gw_ref[r0, k * CW:(k + 1) * CW] = tot.astype(BF16)
            gather_x(k)
            return
        at, to = axes[ROUTE[k][1]]
        tot = s3[k, at].astype(F32)
        for o in range(3):
            tot = tot + r3[k, o].astype(F32)
        r0 = rows(core * 4 + axes[ROUTE[k][0]][0], 32)
        col = pl.ds(pl.multiple_of(k * CW + at * 128, 128), 128)
        gw_ref[r0, col] = tot.astype(BF16)
        for o in (2, 1, 3):
            send(
                gw_ref.at[r0, col], gw_ref.at[r0, col], az_s.at[0], az_r.at[k], (to(o), me)
            )

    def gather_x(k):
        if not WHOLE[k]:
            both(r3.at[k], az_s.at[0], az_r.at[k]).wait_recv()
        at, to = axes[ROUTE[k][0]]
        block = gw_ref.at[rows(core * 4 + at, 32), k * CW:(k + 1) * CW]
        for o in (2, 1, 3):
            send(block, block, ax_s.at[0], ax_r.at[k], (to(o), me))

    def gather_core(k):
        both(r2.at[k], ax_s.at[0], ax_r.at[k]).wait_recv()
        block = gw_ref.at[rows(core, 128), k * CW:(k + 1) * CW]
        send(block, block, ac_s.at[0], ac_r.at[k], (other_core, me))

    def gather_end(k):
        both(r1.at[k], ac_s.at[0], ac_r.at[k]).wait_recv()

    sent.extend([
        both(s4.at[k, 0:3] if WHOLE[k] else r3.at[k], z_s.at[k], z_r.at[k]) for k in range(CHUNKS)
    ])
    sent.extend([
        both(r2, x_s.at[0], x_r.at[0]), both(r3.at[0:WHOLE.count(False)], az_s.at[0], az_r.at[0]), both(r2, ax_s.at[0], ax_r.at[0]),
        both(r1, ac_s.at[0], ac_r.at[0]),
    ])

    weight(0)
    weight(1)
    stage_x(0)
    stage_x(1)
    arrived(1)
    weight(2)
    weight(3)
    mx[...] += nt(w_ref[:, HW:], gall[:, HW:])
    stat2 = all_stats(
        st2, jnp.sum(gt[...] * gain_col * mx[...], axis=0, keepdims=True), st2_s, st2_r
    )
    stage_x(2)
    stage_x(3)
    for k in (0, 1, 3, 2):
        stage_z(k)
    slope = sum_stats(st2, stat2) / INNER
    mixed = mx[...]
    gated = gt[...]
    ng = nt(jnp.ones((8, T), F32), mixed * gated * inv, HI)
    ggt = gain_col * mixed * inv - gated * (inv * inv * inv * slope)
    gz_ref[...] = (ggt * yt[...] * dst[...]).T.astype(BF16)
    yt[...] = ggt * silt[...]

    ws[...] = jnp.zeros_like(ws)
    qs[...] = jnp.zeros_like(qs)
    pr[...] = jnp.zeros_like(pr)
    strict = jnp.where(ri < ci, 1.0, 0.0)

    def back(h):
        c0 = h * HD
        dy = yt[c0:c0 + HD, :]
        xh = xt[c0:c0 + HD, :]
        dyb = dy.astype(BF16)
        for s0, t0 in ((0, 0), (128, 128)):
            dm = tn(xtb[c0:c0 + HD, s0:s0 + 128], dyb[:, t0:])
            qs[s0:s0 + 128, t0:] = (dm * ks[h, s0:s0 + 128, t0:].astype(F32)).astype(BF16)
            ws[s0:s0 + 128, t0:] += dm * hs[h, s0:s0 + 128, t0:]
        top = jnp.sum(nn(qs[0:128, :], tge[...]) * strict[0:128, :], axis=0, keepdims=True)
        low = jnp.sum(
            nn(qs[128:, 128:], tge[128:, 128:]) * strict[128:, 128:], axis=0, keepdims=True
        )
        dld = jnp.concatenate([top[:, 0:128], top[:, 128:] + low], axis=1)
        dxi = nt(dyb, ks[h])
        direct = jnp.sum(xh * dxi, axis=0, keepdims=True) / rw[h:h + 1, :]
        dxt[c0:c0 + HD, :] = dxi + sk_ref[h] * dy
        pr[h:h + 1, :] = jnp.sum(dy * xh, axis=0, keepdims=True)
        pr[4 + h:5 + h, :] = dld
        pr[8 + h:9 + h, :] = direct

    for h in range(NH):
        back(h)

    gather_z(0)
    gather_z(1)
    dld = pr[4:8, :]
    ddt = (pr[8:12, :] - ea * dld) * sig
    gdt_ref[...] = ddt
    pr[4:8, :] = dld * ld
    pr[8:12, :] = ddt

    ones = jnp.ones((8, T), F32)
    pk[...] = jnp.zeros_like(pk)
    pk[0:1, :] = ng[0:1, 0:128]
    pk[1:2, :] = ng[0:1, 128:256]
    for q in range(3):
        pk[2 + q:3 + q, 0:NH] = nt(ones, pr[4 * q:4 * q + 4, :], HI)[0:1, :]
    pc = send(pk, p1, p_s.at[0], p_r.at[0], (other_core, me))

    wb = ws[...].astype(BF16)
    dbc[:, 0:N] = nn(wb, call).astype(BF16)
    dbc[:, N:2 * N] = tn(wb, ball).astype(BF16)
    for d in (4, 3, 5, 2, 6, 1, 7):
        to = (y + d) % NY
        send(dbc.at[rows(to, 32), :], dbr.at[d - 1], db_s.at[0], db_r.at[0], (dp, to * 2 + zh))
    d_all = both(dbr, db_s.at[0], db_r.at[0])
    sent.append(d_all)
    pc.wait_recv()
    p2[xi] = pk[...] + p1[...]
    for o in (1, 2, 3):
        send(p2.at[xi], p2.at[xi], p_s.at[1], p_r.at[1], (at_x(o), me))
    px = both(p2.at[0:3], p_s.at[1], p_r.at[1])
    gather_z(3)
    gather_z(2)
    gather_x(0)
    gather_x(1)
    gx_ref[...] = dxt[...].T.astype(BF16)
    px.wait_recv()
    p3[zl] = p2[0] + p2[1] + p2[2] + p2[3]
    for o in (1, 2, 3):
        send(p3.at[zl], p3.at[zl], p_s.at[2], p_r.at[2], (at_z(o), me))
    pz = both(p3.at[0:3], p_s.at[2], p_r.at[2])
    sent.extend([pc, px, pz])
    d_all.wait_recv()
    tot = dbc[rows(y, 32), :].astype(F32)
    for o in range(NY - 1):
        tot = tot + dbr[o].astype(F32)
    dbp[0] = tot[0:16, :]
    dbp[1] = tot[16:32, :]
    d_last = send(dbp.at[1 - zh], dbq, db_s.at[1], db_r.at[1], (dp, partner))
    sent.append(d_last)
    gather_core(3)
    gather_core(2)
    gather_core(0)
    gather_core(1)
    pz.wait_recv()
    tot = p3[0] + p3[1] + p3[2] + p3[3]
    gn_ref[...] = tot[0:2, :]
    gsk_ref[...] = tot[2, 0:NH]
    gal_ref[...] = tot[3, 0:NH]
    gdb_ref[...] = tot[4, 0:NH]
    d_last.wait_recv()
    tot = dbp[zh] + dbq[...]
    gb_ref[...] = tot[:, 0:N]
    gc_ref[...] = tot[:, N:2 * N]
    for k in range(CHUNKS):
        gather_end(k)
    for copy in sent:
        copy.wait_send()


def finish(*refs):
    n = (len(refs) - 1) // 2
    copies = [pltpu.make_async_copy(refs[i], refs[n + i], refs[-1].at[i]) for i in range(n)]
    for copy in copies:
        copy.start()
    for copy in copies:
        copy.wait()


def per_device(x, z, dt, b, c, a_log, skip, bias, gain, w, g, ids):
    v = pltpu.VMEM
    dma = pltpu.SemaphoreType.DMA
    scratch = [
        v((T, 2 * N), BF16), v((T, DW), BF16), v((NT, 2, 128), F32), v((NT, 2, 128), F32),
        v((CHUNKS, C, CW), BF16), v((CHUNKS, 128, CW), BF16), v((CHUNKS, 128, CW), BF16),
        v((CHUNKS, 3, 32, CW), BF16), v((CHUNKS, 4, 32, 128), BF16), v((CHUNKS, 4, 32, CW), BF16), v((CHUNKS, 3, 32, 128), BF16),
        v((T, 2 * N), BF16), v((NY - 1, 32, 2 * N), BF16), v((2, 16, 2 * N), F32),
        v((16, 2 * N), F32),
        v((8, 128), F32), v((8, 128), F32), v((4, 8, 128), F32), v((4, 8, 128), F32),
        v((T, C), BF16), v((T, C), BF16), v((NH, T), F32), pltpu.SMEM((NH,), F32),
        pltpu.SMEM((NH,), F32), pltpu.SMEM((NH,), F32), v((1, C), F32), v((C, DW), BF16),
        v((1, T), jnp.int32),
        v((16, T), F32), v((16, T), F32), v((T, T), F32), v((T, T), BF16),
        v((C, T), F32), v((C, T), BF16), v((C, T), F32), v((C, T), F32), v((C, T), F32),
        v((C, T), F32), v((NH, T, T), BF16), v((NH, T, T), F32), v((T, T), BF16),
        v((T, T), F32), v((C, T), F32), v((C, T), BF16), v((C, T), F32),
        dma((12,)),
    ]
    counts = [(1, 1), (2, 12), (1, 1), (1, 1)] + [(1, CHUNKS)] * 2 + [(CHUNKS, CHUNKS)] + [(1, CHUNKS)] * 3 + [(2, 2), (3, 3)]
    for n in counts:
        scratch += [dma((n[0],)), dma((n[1],))]
    out = jax.ShapeDtypeStruct
    vmem = pl.BlockSpec(memory_space=pltpu.VMEM)
    anywhere = pl.BlockSpec(memory_space=pl.ANY)
    small = out((NH,), F32)
    results = pl.pallas_call(
        kernel,
        out_shape=(
            out((T, C), BF16), out((T, C), BF16), out((NH, T), F32), out((16, N), F32),
            out((16, N), F32), out((C, DW), BF16), out((2, 128), F32), small, small, small,
        ),
        in_specs=[anywhere] * 12,
        out_specs=(vmem,) * 10,
        scratch_shapes=scratch,
        compiler_params=pltpu.CompilerParams(
            collective_id=0, has_side_effects=True, vmem_limit_bytes=56 * 1024 * 1024
        ),
        cost_estimate=pl.CostEstimate(
            flops=2 * 10**9, bytes_accessed=4 * 2**20, transcendentals=10**6
        ),
    )(x, z, dt, b, c, a_log, skip, bias, gain.reshape(1, C), w, g, ids.reshape(1, T))
    results = pl.pallas_call(
        finish,
        out_shape=tuple(out(r.shape, r.dtype) for r in results),
        in_specs=[vmem] * 10,
        out_specs=(anywhere,) * 10,
        scratch_shapes=[dma((10,))],
    )(*results)
    gx, gz, gdt, gb, gc, gw, gn, gal, gsk, gdb = results
    return gx, gz, gdt, gb, gc, gw, gn.reshape(C), gal, gsk, gdb


def solution(mesh):
    in_specs = (
        P("dp", "tensor"),
        P("dp", "tensor"),
        P("tensor", "dp"),
        P(("dp", "tensor"), None),
        P(("dp", "tensor"), None),
        P("tensor"),
        P("tensor"),
        P("tensor"),
        P("tensor"),
        P("tensor", None),
        P(("dp", "tensor"), None),
        P("dp"),
    )
    out_specs = (
        P("dp", "tensor"),
        P("dp", "tensor"),
        P("tensor", "dp"),
        P(("dp", "tensor"), None),
        P(("dp", "tensor"), None),
        P("tensor", None),
        P("tensor"),
        P("tensor"),
        P("tensor"),
        P("tensor"),
    )
    return jax.shard_map(
        per_device, mesh=mesh, in_specs=in_specs, out_specs=out_specs, check_vma=False
    )
```
